256 devices in a mesh: ulysses: 4 (over x), blk: 32 (over z, y_lo, core), tensor: 2 (over y_hi).
Axes of the slice: x: 4, y: 4 (y_hi: 2, y_lo: 2; y = y_hi * 2 + y_lo), z: 8, core: 2. Of those that a mesh axis runs over, the one named last changes fastest.
Arguments:
- head_inputs: bfloat16 [6144, 3, 32, 128], P(('ulysses', 'blk'), None, 'tensor'), may hold values from -16 to 16
- positions: int32 [3, 6144], P(None, ('ulysses', 'blk')), may hold values from 0 to 51, as said below
- code_words: int32 [4096, 1280], P('tensor'), may hold values from 0 to 65535
- group_scales: bfloat16 [32, 5120], P('tensor'), may hold values from 0.0029907227 to 0.011962891
- out_gate: float32 [5120], P('tensor'), may hold values from 0.5 to 1.5
- out_bias: float32 [5120], P('tensor'), may hold values from -1 to 1
Outputs:
- branch_update: float32 [6144, 5120], P(('ulysses', 'blk'), 'tensor')
The draws below stay inside these ranges and needn't reach their ends.
Inputs may be any that keep to these rules, and one draw needn't show every extreme that they name: `positions`: each token's latent frame, patch row and patch column; no two tokens share a cell of the 4 x 30 x 52 grid, and tokens stand in an arbitrary order.
All inputs are finite; a program needn't handle non-finite values.
Results may differ from the reference program's by a relative error of at most 0.012.
The reference program's roundings to bfloat16 on the way (of `attended` and `weight_table`) count: a program that leaves them out, or rounds other values in their place, can miss the bound.
Values may be sent and summed in bfloat16 or wider, within the bound.
No kernel may reach another device: no remote copies, remote signals or barrier semaphores. Data moves between devices by JAX's collectives and lax.ppermute only.
A program may use at most 128 MiB of HBM per device.

```python
import math
import jax
import jax.numpy as jnp
from jax import lax

D = 5120
HEADS = 32
HD = 128
GROUP = 128
FRAMES = 4
GH = 30
GW = 52
TOKENS = 6144
GROUPS = 32


def draw_head_inputs(key, part):
    key = jax.random.fold_in(key, 7)
    first = jax.random.fold_in(key, 0)
    shape = (TOKENS, 3, HEADS, HD)
    spread = jnp.array([2.5, 1.0, 1.0], jnp.float32).reshape(1, 3, 1, 1)
    result = jnp.clip(jax.random.normal(first, shape, jnp.float32), -6.0, 6.0) * spread
    return result.astype(jnp.bfloat16)


def draw_positions(key, part):
    key = jax.random.fold_in(key, 3)
    first, second = jax.random.split(key, 2)
    cell_count = FRAMES * GH * GW
    others = jax.random.permutation(first, cell_count - 1).astype(jnp.int32)[:TOKENS - 1]
    picked = jnp.concatenate([others, jnp.full((1,), cell_count - 1, jnp.int32)])
    shuffle = jax.random.permutation(second, TOKENS).astype(jnp.int32)
    order = picked[shuffle]
    plane_cells = GH * GW
    grid_frame = order // plane_cells
    grid_row = order // GW % GH
    grid_column = order % GW
    return jnp.stack([grid_frame, grid_row, grid_column]).astype(jnp.int32)


def with_ends(drawn, rng, smallest, largest):
    longest = drawn.shape.index(max(drawn.shape))
    spots = []
    for shift in (0, 1):
        where = [jax.random.randint(jax.random.fold_in(rng, axis), (), 0, length) for axis, length in enumerate(drawn.shape)]
        where[longest] = (where[longest] + shift) % drawn.shape[longest]
        spots.append(tuple(where))
    return drawn.at[spots[0]].set(smallest).at[spots[1]].set(largest)


def level_of(rng, shape, cuts, smallest, high):
    def one(position, blocks):
        draws = jax.random.uniform(jax.random.fold_in(jax.random.fold_in(rng, 6), position), (blocks,), jnp.float32, smallest / len(cuts), high / len(cuts))
        return jnp.repeat(jnp.exp(draws), shape[position] // blocks).reshape((-1,) + (1,) * (len(shape) - position - 1))

    level = one(*cuts[0])
    for cut in cuts[1:]:
        level = level * one(*cut)
    return level


def gaussian(rng, shape, scale, limit, cuts=(), held_as=jnp.bfloat16):
    drawn = scale * jax.random.normal(rng, shape, jnp.float32)
    if cuts:
        drawn = drawn * level_of(rng, shape, cuts, -0.22, 0.18)
    return jnp.clip(drawn, -limit, limit).astype(held_as)


def setup_inputs(seed: int = 0) -> dict:
    key_of = jax.random.split(jax.random.key(seed), 7)
    return {
        "head_inputs": draw_head_inputs(jax.random.fold_in(key_of[6], 71), 0),
        "positions": draw_positions(jax.random.fold_in(key_of[6], 71), 0),
        "code_words": with_ends(jax.random.randint(key_of[2], (HEADS * HD, D // 4), 0, 65536), jax.random.fold_in(key_of[2], 1), 0, 65535).astype(jnp.int32),
        "group_scales": jnp.clip(jnp.exp(math.log(0.011962891) - 1.3862944 * jax.random.uniform(key_of[3], (GROUPS, D), jnp.float32) ** level_of(key_of[3], (GROUPS, D), ((0, 2),), -0.2, 0.2)), 0.0029907227, 0.011962891).astype(jnp.bfloat16),
        "out_gate": jnp.clip(0.5 + 1.0 * jax.random.uniform(key_of[4], (D,), jnp.float32) ** level_of(key_of[4], (D,), ((0, 2),), -0.2, 0.2), 0.5, 1.5),
        "out_bias": gaussian(key_of[5], (D,), 0.2, 1.0, ((0, 2),), jnp.float32),
    }


def rope_tables(positions, width):
    pair_index = jnp.arange(width, dtype=jnp.int32) // 2
    frame_pairs = (width - 4 * (width // 6)) // 2
    side_pairs = width // 6
    segment = jnp.where(pair_index < frame_pairs, 0, jnp.where(pair_index < frame_pairs + side_pairs, 1, 2))
    offset = jnp.where(segment == 0, 0, jnp.where(segment == 1, frame_pairs, frame_pairs + side_pairs))
    within = (pair_index - offset).astype(jnp.float32)
    extent = jnp.where(segment == 0, frame_pairs, side_pairs).astype(jnp.float32)
    frequency = jnp.power(jnp.float32(10000.0), -within / extent)
    coords = positions.astype(jnp.float32)
    chosen = coords[0][:, None] * (segment == 0).astype(jnp.float32)[None, :] + coords[1][:, None] * (segment == 1).astype(jnp.float32)[None, :] + coords[2][:, None] * (segment == 2).astype(jnp.float32)[None, :]
    angles = chosen * frequency[None, :]
    return (jnp.cos(angles), jnp.sin(angles))

def pair_swap(width):
    source = lax.broadcasted_iota(jnp.int32, (width, width), 0)
    target = lax.broadcasted_iota(jnp.int32, (width, width), 1)
    is_even = target % 2 == 0
    return jnp.where(is_even & (source == target + 1), -1.0, jnp.where(~is_even & (source == target - 1), 1.0, 0.0)).astype(jnp.float32)

def rotate(inputs, cosine, sine):
    width = inputs.shape[-1]
    turned = jnp.dot(inputs.reshape(-1, width), pair_swap(width), precision=lax.Precision.HIGHEST).reshape(inputs.shape)
    return inputs * cosine[:, None, :] + turned * sine[:, None, :]

def dequantize(code_words, group_scales, group_rows):
    levels = jnp.concatenate([jnp.bitwise_and(jnp.right_shift(code_words, 4 * shift_count), 15) for shift_count in range(4)], axis=1)
    levels = (levels - 8).astype(jnp.float32)
    spread_scales = jnp.repeat(group_scales.astype(jnp.float32), group_rows, axis=0)
    return (levels * spread_scales).astype(jnp.bfloat16)

def reference(head_inputs, positions, code_words, group_scales, out_gate, out_bias):
    cosine, sine = rope_tables(positions, HD)
    queries = rotate(head_inputs[:, 0].astype(jnp.float32), cosine, sine).astype(jnp.bfloat16)
    keys_all = rotate(head_inputs[:, 1].astype(jnp.float32), cosine, sine).astype(jnp.bfloat16)
    values_all = head_inputs[:, 2]
    scale_factor = 1.0 / math.sqrt(HD)
    block_count = 8
    block_rows = TOKENS // block_count

    def per_head(stacked):
        head_queries, head_keys, head_values = stacked

        def per_block(query_block):
            scores = jnp.dot(query_block, head_keys.T, preferred_element_type=jnp.float32) * scale_factor
            row_peak = lax.optimization_barrier(jnp.max(scores, axis=1, keepdims=True))
            lifted = jnp.exp(scores - row_peak)
            totals = lax.optimization_barrier(jnp.sum(lifted, axis=1, keepdims=True))
            mixed = jnp.dot(lifted.astype(jnp.bfloat16), head_values, preferred_element_type=jnp.float32)
            return (mixed / totals).astype(jnp.bfloat16)
        result = lax.map(per_block, head_queries.reshape(block_count, block_rows, HD))
        return result.reshape(TOKENS, HD)
    attended = lax.map(per_head, (jnp.transpose(queries, (1, 0, 2)), jnp.transpose(keys_all, (1, 0, 2)), jnp.transpose(values_all, (1, 0, 2))))
    flat_rows = jnp.transpose(attended, (1, 0, 2)).reshape(TOKENS, HEADS * HD)
    weight_table = dequantize(code_words, group_scales, GROUP)
    projected = jnp.dot(flat_rows, weight_table, preferred_element_type=jnp.float32)
    return out_gate[None, :] * (projected + out_bias[None, :])
```

```python
import functools
import math

import jax
import jax.numpy as jnp
import numpy as np
from jax import lax
from jax.experimental import pallas as pl
from jax.experimental.pallas import tpu as pltpu
from jax.sharding import Mesh
from jax.sharding import PartitionSpec as P

HD = 128
LOG2E = 1.4426950408889634
F32 = jnp.float32
BF16 = jnp.bfloat16


def frequency_table(width):
    pair = np.arange(width) // 2
    frame = (width - 4 * (width // 6)) // 2
    side = width // 6
    segment = np.where(pair < frame, 0, np.where(pair < frame + side, 1, 2))
    start = np.where(segment == 0, 0, np.where(segment == 1, frame, frame + side))
    extent = np.where(segment == 0, frame, side)
    value = np.power(10000.0, -(pair - start) / extent)
    return np.stack([np.where(segment == s, value, 0.0) for s in range(3)]).astype(np.float32)


def rotate_kernel(pos_ref, freq_ref, x_ref, out_ref, wide):
    tokens, kinds, heads, width = x_ref.shape
    pos = pos_ref[...].astype(F32)
    freq = freq_ref[...]
    angles = pos[:, 0:1] * freq[0:1, :] + pos[:, 1:2] * freq[1:2, :] + pos[:, 2:3] * freq[2:3, :]
    cosine = jnp.cos(angles)
    sine = jnp.sin(angles)
    lane = lax.broadcasted_iota(jnp.int32, (tokens, width), 1)
    is_even = lane % 2 == 0
    sine_even = jnp.where(is_even, -sine, 0.0)
    sine_odd = jnp.where(is_even, 0.0, sine)
    wide[...] = x_ref[...].astype(F32).reshape(tokens * kinds * heads, width)
    for kind in range(kinds):
        for head in range(heads):
            x = wide[pl.ds(kind * heads + head, tokens, stride=kinds * heads), :]
            if kind < 2:
                right = pltpu.roll(x, 1, 1)
                left = pltpu.roll(x, width - 1, 1)
                x = x * cosine + (left * sine_even + right * sine_odd)
            out_ref[head, kind] = x.astype(BF16)


def rotate(positions, head_inputs):
    tokens, kinds, heads, width = head_inputs.shape
    return pl.pallas_call(
        rotate_kernel,
        out_shape=jax.ShapeDtypeStruct((heads, kinds, tokens, width), BF16),
        scratch_shapes=[pltpu.VMEM((tokens * kinds * heads, width), F32)],
        compiler_params=pltpu.CompilerParams(vmem_limit_bytes=16 * 1024 * 1024),
    )(positions.T, jnp.asarray(frequency_table(width)), head_inputs)


def dequantize_kernel(half_ref, words_ref, scales_ref, out_ref):
    half = half_ref[0]
    quarter = words_ref.shape[1]
    words = words_ref[...]
    for part in range(2):
        mine = half if part else 1 - half
        shifted = lax.shift_right_logical(words, jnp.full(words.shape, 8 * mine, jnp.int32))
        for low in range(2):
            scale = scales_ref[0, pl.ds(2 * mine + low, 1), :]
            if low:
                level = ((shifted & 240) - 128).astype(F32) * (scale * 0.0625)
            else:
                level = ((shifted & 15) - 8).astype(F32) * scale
            out_ref[part, :, low * quarter : (low + 1) * quarter] = level.astype(BF16)


def dequantize(half, code_words, group_scales):
    rows, quarter = code_words.shape
    groups = group_scales.shape[0]
    depth = rows // groups
    scales = group_scales.astype(F32).reshape(groups, 4, quarter)
    return pl.pallas_call(
        dequantize_kernel,
        grid=(groups,),
        in_specs=[
            pl.BlockSpec(memory_space=pltpu.SMEM),
            pl.BlockSpec((depth, quarter), lambda g: (g, 0)),
            pl.BlockSpec((1, 4, quarter), lambda g: (g, 0, 0)),
        ],
        out_specs=pl.BlockSpec((2, depth, 2 * quarter), lambda g: (0, g, 0)),
        out_shape=jax.ShapeDtypeStruct((2, rows, 2 * quarter), BF16),
        compiler_params=pltpu.CompilerParams(vmem_limit_bytes=24 * 1024 * 1024),
        cost_estimate=pl.CostEstimate(flops=rows * quarter * 30, bytes_accessed=rows * quarter * 12, transcendentals=0),
    )(half, code_words, scales)


def attend_kernel(first, last, blocks, tile, q_ref, *refs):
    kv_refs = refs[:blocks]
    refs = refs[blocks:]
    if not first:
        m_in, l_in, acc_in = refs[:3]
        refs = refs[3:]
    scale = LOG2E / math.sqrt(HD)
    groups, _, rows, width = q_ref.shape
    total = groups * rows
    queries = q_ref[:, 0].reshape(total, width)
    keys, values = [], []
    for ref in kv_refs:
        at = ref.shape[1] - 2
        keys.append(ref[:, at].reshape(total, width))
        values.append(ref[:, at + 1].reshape(total, width))

    def scores(step):
        row, block = divmod(step, blocks)
        return lax.dot_general(
            queries[row * tile : (row + 1) * tile],
            keys[block],
            (((1,), (1,)), ((), ())),
            preferred_element_type=F32,
        )

    steps = (total // tile) * blocks
    ahead = scores(0)
    for step in range(steps):
        row, block = divmod(step, blocks)
        here = slice(row * tile, (row + 1) * tile)
        s = ahead
        if step + 1 < steps:
            ahead = scores(step + 1)
        fresh = first and block == 0
        if block == 0 and not first:
            peak, total_l, acc = m_in[here, :], l_in[here, :], acc_in[here, :]
        s_peak = jnp.broadcast_to(jnp.max(s, axis=1, keepdims=True), (tile, width))
        new_peak = s_peak if fresh else jnp.maximum(peak, s_peak)
        parts, part_sum = [], None
        for lane in range(total // width):
            lifted = jnp.exp2((s[:, lane * width : (lane + 1) * width] - new_peak) * scale)
            part_sum = lifted if part_sum is None else part_sum + lifted
            parts.append(lifted.astype(BF16))
        mixed = jnp.dot(jnp.concatenate(parts, axis=1), values[block], preferred_element_type=F32)
        if fresh:
            total_l, acc = part_sum, mixed
        else:
            fade = jnp.exp2((peak - new_peak) * scale)
            total_l = total_l * fade + part_sum
            acc = acc * fade + mixed
        peak = new_peak
        if block == blocks - 1:
            if last:
                (out_ref,) = refs
                whole = jnp.sum(total_l, axis=1, keepdims=True)
                out_ref[here, :] = (acc / whole).astype(BF16)
            else:
                m_out, l_out, acc_out = refs
                m_out[here, :] = peak
                l_out[here, :] = total_l
                acc_out[here, :] = acc


def attend(queries, kv_blocks, state, last, tile=128):
    groups, _, rows, width = queries.shape
    total = groups * rows
    blocks = len(kv_blocks)
    first = state is None
    carried = jax.ShapeDtypeStruct((total, width), F32)
    out_shape = jax.ShapeDtypeStruct((total, width), BF16) if last else (carried,) * 3
    pairs = total * total * blocks
    return pl.pallas_call(
        functools.partial(attend_kernel, first, last, blocks, tile),
        out_shape=out_shape,
        compiler_params=pltpu.CompilerParams(vmem_limit_bytes=32 * 1024 * 1024),
        cost_estimate=pl.CostEstimate(
            flops=pairs * width * 4, bytes_accessed=total * width * 2 * (2 * blocks + 7), transcendentals=pairs
        ),
    )(queries, *kv_blocks, *(() if first else state))


def project_kernel(x_ref, w_ref, out_ref):
    heads = x_ref.shape[0]
    x = jnp.concatenate([x_ref[h] for h in range(heads)], axis=1)
    out_ref[...] = jnp.dot(x, w_ref[0], preferred_element_type=F32).astype(out_ref.dtype)


def project(part, returned, weights, out_type, tile=512):
    heads, tokens, width = returned.shape
    _, rows, columns = weights.shape
    return pl.pallas_call(
        project_kernel,
        grid=(columns // tile,),
        in_specs=[
            pl.BlockSpec((heads, tokens, width), lambda c: (0, 0, 0)),
            pl.BlockSpec((1, rows, tile), lambda c: (part, 0, c)),
        ],
        out_specs=pl.BlockSpec((tokens, tile), lambda c: (0, c)),
        out_shape=jax.ShapeDtypeStruct((tokens, columns), out_type),
        compiler_params=pltpu.CompilerParams(vmem_limit_bytes=24 * 1024 * 1024),
        cost_estimate=pl.CostEstimate(
            flops=2 * tokens * rows * columns, bytes_accessed=rows * columns * 2, transcendentals=0
        ),
    )(returned, weights)


HEAD_AXES = ("x", "zl", "yl")


def body(head_inputs, positions, code_words, group_scales, out_gate, out_bias):
    ring = lax.axis_size("zh")
    half = lax.axis_index("yh").astype(jnp.int32).reshape(1)
    prepared = rotate(positions, head_inputs)
    grouped = lax.all_to_all(prepared, HEAD_AXES, split_axis=0, concat_axis=0, tiled=True)
    own = grouped[:, 1:]

    def swap(a):
        return lax.ppermute(a, "c", [(0, 1), (1, 0)])

    up = lax.ppermute(own, "zh", [(i, (i + 1) % ring) for i in range(ring)])
    down = lax.ppermute(own, "zh", [(i, (i - 1) % ring) for i in range(ring)])
    beside = swap(own)
    weights = dequantize(half, code_words, group_scales)
    state = attend(grouped, [grouped, beside], None, False)
    core = lax.axis_index("c")
    onward = jnp.where(core == 0, up, down)
    hops = []
    for i in range(ring):
        hops.append((2 * i, 2 * ((i + 1) % ring)))
        hops.append((2 * i + 1, 2 * ((i - 1) % ring) + 1))
    far = lax.ppermute(onward, ("zh", "c"), hops)
    up_beside, down_beside = swap(up), swap(down)
    state = attend(grouped, [up, down], state, False)
    state = attend(grouped, [up_beside, down_beside], state, False)
    far_beside = swap(far)
    attended = attend(grouped, [far, far_beside], state, True)
    chunks = prepared.shape[0]
    returned = lax.all_to_all(
        attended.reshape(chunks, -1, HD), HEAD_AXES, split_axis=0, concat_axis=0, tiled=True
    )
    outgoing = project(0, returned, weights, BF16)
    incoming = lax.ppermute(outgoing, "yh", [(0, 1), (1, 0)])
    kept = project(1, returned, weights, F32)
    return out_gate[None, :] * (kept + incoming.astype(F32) + out_bias[None, :])


def solution(mesh):
    x, blk, yh = mesh.devices.shape
    fine = Mesh(mesh.devices.reshape(x, blk // 8, 2, 2, 2, yh), ("x", "zh", "zl", "yl", "c", "yh"))
    tokens = ("x", "zh", "zl", "yl", "c")
    placed = (
        P(tokens, None, "yh", None),
        P(None, tokens),
        P("yh", None),
        P("yh", None),
        P("yh"),
        P("yh"),
    )
    return jax.shard_map(
        body, mesh=fine, in_specs=placed, out_specs=P(tokens, "yh"), check_vma=False
    )
```

```python
import functools
import math

import jax
import jax.numpy as jnp
import numpy as np
from jax import lax
from jax.experimental import pallas as pl
from jax.experimental.pallas import tpu as pltpu
from jax.sharding import Mesh
from jax.sharding import PartitionSpec as P

HD = 128
LOG2E = 1.4426950408889634
F32 = jnp.float32
BF16 = jnp.bfloat16


def frequency_table(width):
    pair = np.arange(width) // 2
    frame = (width - 4 * (width // 6)) // 2
    side = width // 6
    segment = np.where(pair < frame, 0, np.where(pair < frame + side, 1, 2))
    start = np.where(segment == 0, 0, np.where(segment == 1, frame, frame + side))
    extent = np.where(segment == 0, frame, side)
    value = np.power(10000.0, -(pair - start) / extent)
    return np.stack([np.where(segment == s, value, 0.0) for s in range(3)]).astype(np.float32)


def rotate_kernel(pos_ref, freq_ref, x_ref, out_ref, wide):
    tokens, kinds, heads, width = x_ref.shape
    angles = lax.dot_general(
        pos_ref[...].astype(F32),
        freq_ref[...],
        (((0,), (0,)), ((), ())),
        precision=lax.Precision.HIGHEST,
        preferred_element_type=F32,
    )
    cosine = jnp.cos(angles)
    sine = jnp.sin(angles)
    lane = lax.broadcasted_iota(jnp.int32, (tokens, width), 1)
    is_even = lane % 2 == 0
    sine_even = jnp.where(is_even, -sine, 0.0)
    sine_odd = jnp.where(is_even, 0.0, sine)
    wide[...] = x_ref[...].astype(F32).reshape(tokens * kinds * heads, width)
    for kind in range(kinds):
        for head in range(heads):
            x = wide[pl.ds(kind * heads + head, tokens, stride=kinds * heads), :]
            if kind < 2:
                right = pltpu.roll(x, 1, 1)
                left = pltpu.roll(x, width - 1, 1)
                x = x * cosine + (left * sine_even + right * sine_odd)
            out_ref[head, kind] = x.astype(BF16)


def rotate(positions, head_inputs):
    tokens, kinds, heads, width = head_inputs.shape
    return pl.pallas_call(
        rotate_kernel,
        out_shape=jax.ShapeDtypeStruct((heads, kinds, tokens, width), BF16),
        scratch_shapes=[pltpu.VMEM((tokens * kinds * heads, width), F32)],
        compiler_params=pltpu.CompilerParams(vmem_limit_bytes=16 * 1024 * 1024),
    )(positions, jnp.asarray(frequency_table(width)), head_inputs)


def dequantize_kernel(half_ref, words_ref, scales_ref, out_ref):
    half = half_ref[0]
    quarter = words_ref.shape[1]
    words = words_ref[...]
    for part in range(2):
        mine = half if part else 1 - half
        shifted = lax.shift_right_logical(words, jnp.full(words.shape, 8 * mine, jnp.int32))
        for low in range(2):
            scale = scales_ref[0, pl.ds(2 * mine + low, 1), :]
            if low:
                level = ((shifted & 240) - 128).astype(F32) * (scale * 0.0625)
            else:
                level = ((shifted & 15) - 8).astype(F32) * scale
            out_ref[part, :, low * quarter : (low + 1) * quarter] = level.astype(BF16)


def dequantize(half, code_words, group_scales):
    rows, quarter = code_words.shape
    groups = group_scales.shape[0]
    depth = rows // groups
    scales = group_scales.astype(F32).reshape(groups, 4, quarter)
    return pl.pallas_call(
        dequantize_kernel,
        grid=(groups,),
        in_specs=[
            pl.BlockSpec(memory_space=pltpu.SMEM),
            pl.BlockSpec((depth, quarter), lambda g: (g, 0)),
            pl.BlockSpec((1, 4, quarter), lambda g: (g, 0, 0)),
        ],
        out_specs=pl.BlockSpec((2, depth, 2 * quarter), lambda g: (0, g, 0)),
        out_shape=jax.ShapeDtypeStruct((2, rows, 2 * quarter), BF16),
        compiler_params=pltpu.CompilerParams(vmem_limit_bytes=24 * 1024 * 1024),
        cost_estimate=pl.CostEstimate(flops=rows * quarter * 30, bytes_accessed=rows * quarter * 12, transcendentals=0),
    )(half, code_words, scales)


def attend_kernel(first, last, blocks, tile, q_ref, *refs):
    kv_refs = refs[:blocks]
    refs = refs[blocks:]
    if not first:
        m_in, l_in, acc_in = refs[:3]
        refs = refs[3:]
    scale = LOG2E / math.sqrt(HD)
    groups, _, rows, width = q_ref.shape
    total = groups * rows
    queries = q_ref[:, 0].reshape(total, width)
    keys, values = [], []
    for ref in kv_refs:
        at = ref.shape[1] - 2
        keys.append(ref[:, at].reshape(total, width))
        values.append(ref[:, at + 1].reshape(total, width))

    def scores(step):
        row, block = divmod(step, blocks)
        return lax.dot_general(
            queries[row * tile : (row + 1) * tile],
            keys[block],
            (((1,), (1,)), ((), ())),
            preferred_element_type=F32,
        )

    steps = (total // tile) * blocks
    ahead = scores(0)
    for step in range(steps):
        row, block = divmod(step, blocks)
        here = slice(row * tile, (row + 1) * tile)
        s = ahead
        if step + 1 < steps:
            ahead = scores(step + 1)
        fresh = first and block == 0
        if block == 0 and not first:
            peak, total_l, acc = m_in[here, :], l_in[here, :], acc_in[here, :]
        s_peak = jnp.broadcast_to(jnp.max(s, axis=1, keepdims=True), (tile, width))
        new_peak = s_peak if fresh else jnp.maximum(peak, s_peak)
        parts, part_sum = [], None
        for lane in range(total // width):
            lifted = jnp.exp2((s[:, lane * width : (lane + 1) * width] - new_peak) * scale)
            part_sum = lifted if part_sum is None else part_sum + lifted
            parts.append(lifted.astype(BF16))
        mixed = jnp.dot(jnp.concatenate(parts, axis=1), values[block], preferred_element_type=F32)
        if fresh:
            total_l, acc = part_sum, mixed
        else:
            fade = jnp.exp2((peak - new_peak) * scale)
            total_l = total_l * fade + part_sum
            acc = acc * fade + mixed
        peak = new_peak
        if block == blocks - 1:
            if last:
                (out_ref,) = refs
                whole = jnp.sum(total_l, axis=1, keepdims=True)
                out_ref[here, :] = (acc / whole).astype(BF16)
            else:
                m_out, l_out, acc_out = refs
                m_out[here, :] = peak
                l_out[here, :] = total_l
                acc_out[here, :] = acc


def attend(queries, kv_blocks, state, last, tile=128):
    groups, _, rows, width = queries.shape
    total = groups * rows
    blocks = len(kv_blocks)
    first = state is None
    carried = jax.ShapeDtypeStruct((total, width), F32)
    out_shape = jax.ShapeDtypeStruct((total, width), BF16) if last else (carried,) * 3
    pairs = total * total * blocks
    return pl.pallas_call(
        functools.partial(attend_kernel, first, last, blocks, tile),
        out_shape=out_shape,
        compiler_params=pltpu.CompilerParams(vmem_limit_bytes=16 * 1024 * 1024),
        cost_estimate=pl.CostEstimate(
            flops=pairs * width * 4, bytes_accessed=total * width * 2 * (2 * blocks + 7), transcendentals=pairs
        ),
    )(queries, *kv_blocks, *(() if first else state))


def project_kernel(x_ref, w_ref, out_ref):
    heads = x_ref.shape[0]
    x = jnp.concatenate([x_ref[h] for h in range(heads)], axis=1)
    out_ref[...] = jnp.dot(x, w_ref[0], preferred_element_type=F32).astype(out_ref.dtype)


def project(part, returned, weights, out_type, tile=512):
    heads, tokens, width = returned.shape
    _, rows, columns = weights.shape
    return pl.pallas_call(
        project_kernel,
        grid=(columns // tile,),
        in_specs=[
            pl.BlockSpec((heads, tokens, width), lambda c: (0, 0, 0)),
            pl.BlockSpec((1, rows, tile), lambda c: (part, 0, c)),
        ],
        out_specs=pl.BlockSpec((tokens, tile), lambda c: (0, c)),
        out_shape=jax.ShapeDtypeStruct((tokens, columns), out_type),
        compiler_params=pltpu.CompilerParams(vmem_limit_bytes=24 * 1024 * 1024),
        cost_estimate=pl.CostEstimate(
            flops=2 * tokens * rows * columns, bytes_accessed=rows * columns * 2, transcendentals=0
        ),
    )(returned, weights)


HEAD_AXES = ("x", "zl", "yl")
RING = "zh"


def body(head_inputs, positions, code_words, group_scales, out_gate, out_bias):
    ring = lax.axis_size(RING)
    half = lax.axis_index("yh").astype(jnp.int32).reshape(1)
    prepared = rotate(positions, head_inputs)
    grouped = lax.all_to_all(prepared, HEAD_AXES, split_axis=0, concat_axis=0, tiled=True)
    own = grouped[:, 1:]

    def swap(a):
        return lax.ppermute(a, "c", [(0, 1), (1, 0)])

    up = lax.ppermute(own, RING, [(i, (i + 1) % ring) for i in range(ring)])
    down = lax.ppermute(own, RING, [(i, (i - 1) % ring) for i in range(ring)])
    beside = swap(own)
    weights = dequantize(half, code_words, group_scales)
    state = attend(grouped, [grouped, beside], None, False)
    up, down, state, weights = lax.optimization_barrier((up, down, state, weights))
    core = lax.axis_index("c")
    hops = []
    for i in range(ring):
        hops.append((2 * i, 2 * ((i + 1) % ring)))
        hops.append((2 * i + 1, 2 * ((i - 1) % ring) + 1))
    far = lax.ppermute(jnp.where(core == 0, up, down), (RING, "c"), hops)
    up_beside, down_beside = swap(up), swap(down)
    state = attend(grouped, [up, down], state, False)
    state = attend(grouped, [up_beside, down_beside], state, False)
    far, state = lax.optimization_barrier((far, state))
    far_beside = swap(far)
    attended = attend(grouped, [far, far_beside], state, True)
    chunks = prepared.shape[0]
    returned = lax.all_to_all(
        attended.reshape(chunks, -1, HD), HEAD_AXES, split_axis=0, concat_axis=0, tiled=True
    )
    outgoing = project(0, returned, weights, BF16)
    incoming = lax.ppermute(outgoing, "yh", [(0, 1), (1, 0)])
    kept = project(1, returned, weights, F32)
    return out_gate[None, :] * (kept + incoming.astype(F32) + out_bias[None, :])


def solution(mesh):
    x, blk, yh = mesh.devices.shape
    fine = Mesh(mesh.devices.reshape(x, blk // 8, 2, 2, 2, yh), ("x", "zh", "zl", "yl", "c", "yh"))
    tokens = ("x", "zh", "zl", "yl", "c")
    placed = (
        P(tokens, None, "yh", None),
        P(None, tokens),
        P("yh", None),
        P("yh", None),
        P("yh"),
        P("yh"),
    )
    return jax.shard_map(
        body, mesh=fine, in_specs=placed, out_specs=P(tokens, "yh"), check_vma=False
    )
```

```python
import functools
import math

import jax
import jax.numpy as jnp
from jax import lax
from jax.experimental import pallas as pl
from jax.experimental.pallas import tpu as pltpu
from jax.sharding import Mesh
from jax.sharding import PartitionSpec as P

HD = 128
LOG2E = 1.4426950408889634
F32 = jnp.float32
BF16 = jnp.bfloat16


def angle_rates(width):
    frame = (width - 4 * (width // 6)) // 2
    side = width // 6
    pair = lax.broadcasted_iota(jnp.int32, (3, width), 1) // 2
    row = lax.broadcasted_iota(jnp.int32, (3, width), 0)
    start = jnp.where(row == 0, 0, jnp.where(row == 1, frame, frame + side))
    extent = jnp.where(row == 0, frame, side)
    within = pair - start
    rate = jnp.exp(within.astype(F32) / extent.astype(F32) * (-math.log(10000.0)))
    return jnp.where((within >= 0) & (within < extent), rate, 0.0)


def rotate_kernel(pos_hbm, x_hbm, out_ref, pos_ref, x_ref, wide, sems):
    pos_copy = pltpu.make_async_copy(pos_hbm, pos_ref, sems.at[0])
    x_copy = pltpu.make_async_copy(x_hbm, x_ref, sems.at[1])
    pos_copy.start()
    x_copy.start()
    tokens, kinds, heads, width = x_ref.shape
    rates = angle_rates(width)
    is_even = lax.broadcasted_iota(jnp.int32, (tokens, width), 1) % 2 == 0
    pos_copy.wait()
    angles = lax.dot_general(
        pos_ref[...].astype(F32),
        rates,
        (((0,), (0,)), ((), ())),
        precision=lax.Precision.HIGHEST,
        preferred_element_type=F32,
    )
    cosine = jnp.cos(angles)
    sine = jnp.sin(angles)
    sine_even = jnp.where(is_even, -sine, 0.0)
    sine_odd = jnp.where(is_even, 0.0, sine)
    x_copy.wait()
    wide[...] = x_ref[...].astype(F32).reshape(tokens * kinds * heads, width)
    for kind in range(kinds):
        for head in range(heads):
            x = wide[pl.ds(kind * heads + head, tokens, stride=kinds * heads), :]
            if kind < 2:
                right = pltpu.roll(x, 1, 1)
                left = pltpu.roll(x, width - 1, 1)
                x = x * cosine + (left * sine_even + right * sine_odd)
            out_ref[head, kind] = x.astype(BF16)


def rotate(positions, head_inputs):
    tokens, kinds, heads, width = head_inputs.shape
    return pl.pallas_call(
        rotate_kernel,
        in_specs=[pl.BlockSpec(memory_space=pltpu.HBM)] * 2,
        out_specs=pl.BlockSpec(memory_space=pltpu.VMEM),
        out_shape=jax.ShapeDtypeStruct((heads, kinds, tokens, width), BF16),
        scratch_shapes=[
            pltpu.VMEM(positions.shape, positions.dtype),
            pltpu.VMEM(head_inputs.shape, head_inputs.dtype),
            pltpu.VMEM((tokens * kinds * heads, width), F32),
            pltpu.SemaphoreType.DMA((2,)),
        ],
        compiler_params=pltpu.CompilerParams(vmem_limit_bytes=16 * 1024 * 1024),
    )(in_hbm(positions), in_hbm(head_inputs))


def in_hbm(array):
    return pltpu.with_memory_space_constraint(array, pltpu.HBM)


def dequantize_kernel(half_ref, words_ref, scales_ref, out_ref, slots, wide, sems):
    rows, quarter = words_ref.shape
    groups = scales_ref.shape[0]
    depth = rows // groups
    half = half_ref[0]
    ahead, chunk, across = slots.shape[0], 16, 256

    def fetch(g):
        slot = lax.rem(g, ahead)
        start = pl.multiple_of(g * depth, depth)
        return pltpu.make_async_copy(words_ref.at[pl.ds(start, depth)], slots.at[slot], sems.at[slot])

    for g in range(ahead):
        fetch(g).start()
    wide[...] = scales_ref[...].astype(F32)

    def step(g, carry):
        fetch(g).wait()
        slot = lax.rem(g, ahead)
        start = pl.multiple_of(g * depth, depth)
        for column in range(0, quarter, across):
            for part in range(2):
                mine = half if part else 1 - half
                scales = []
                for low in range(2):
                    at = pl.multiple_of((2 * mine + low) * quarter + column, 128)
                    row = wide[pl.ds(g, 1), pl.ds(at, across)] * (0.0625 if low else 1.0)
                    scales.append(jnp.broadcast_to(row, (chunk, across)))
                for r in range(0, depth, chunk):
                    words = slots[slot, r : r + chunk, column : column + across]
                    shifted = lax.shift_right_logical(words, jnp.full(words.shape, 8 * mine, jnp.int32))
                    for low in range(2):
                        level = ((shifted & 240) - 128) if low else ((shifted & 15) - 8)
                        out_ref[
                            part,
                            pl.ds(start + r, chunk),
                            low * quarter + column : low * quarter + column + across,
                        ] = (level.astype(F32) * scales[low]).astype(BF16)

        @pl.when(g + ahead < groups)
        def _():
            fetch(g + ahead).start()

        return carry

    lax.fori_loop(0, groups, step, 0)


def dequantize(half, code_words, group_scales):
    rows, quarter = code_words.shape
    groups = group_scales.shape[0]
    ahead = 4
    return pl.pallas_call(
        dequantize_kernel,
        in_specs=[
            pl.BlockSpec(memory_space=pltpu.SMEM),
            pl.BlockSpec(memory_space=pltpu.HBM),
            pl.BlockSpec(memory_space=pltpu.VMEM),
        ],
        out_specs=pl.BlockSpec(memory_space=pltpu.VMEM),
        out_shape=pltpu.VMEM((2, rows, 2 * quarter), BF16),
        scratch_shapes=[
            pltpu.VMEM((ahead, rows // groups, quarter), jnp.int32),
            pltpu.VMEM(group_scales.shape, F32),
            pltpu.SemaphoreType.DMA((ahead,)),
        ],
        compiler_params=pltpu.CompilerParams(vmem_limit_bytes=8 * 1024 * 1024),
        cost_estimate=pl.CostEstimate(flops=rows * quarter * 30, bytes_accessed=rows * quarter * 12, transcendentals=0),
    )(half, in_hbm(code_words), group_scales)


def attend_kernel(first, last, blocks, tile, q_ref, *refs):
    kv_refs = refs[:blocks]
    refs = refs[blocks:]
    if not first:
        m_in, l_in, acc_in = refs[:3]
        refs = refs[3:]
    scale = LOG2E / math.sqrt(HD)
    groups, _, rows, width = q_ref.shape
    total = groups * rows
    queries = q_ref[:, 0].reshape(total, width)
    keys, values = [], []
    for ref in kv_refs:
        at = ref.shape[1] - 2
        keys.append(ref[:, at].reshape(total, width))
        values.append(ref[:, at + 1].reshape(total, width))

    def scores(step):
        row, block = divmod(step, blocks)
        return lax.dot_general(
            queries[row * tile : (row + 1) * tile],
            keys[block],
            (((1,), (1,)), ((), ())),
            preferred_element_type=F32,
        )

    steps = (total // tile) * blocks
    ahead = scores(0)
    for step in range(steps):
        row, block = divmod(step, blocks)
        here = slice(row * tile, (row + 1) * tile)
        s = ahead
        if step + 1 < steps:
            ahead = scores(step + 1)
        fresh = first and block == 0
        if block == 0 and not first:
            peak, total_l, acc = m_in[here, :], l_in[here, :], acc_in[here, :]
        s_peak = jnp.broadcast_to(jnp.max(s, axis=1, keepdims=True), (tile, width))
        new_peak = s_peak if fresh else jnp.maximum(peak, s_peak)
        parts, part_sum = [], None
        for lane in range(total // width):
            lifted = jnp.exp2((s[:, lane * width : (lane + 1) * width] - new_peak) * scale)
            part_sum = lifted if part_sum is None else part_sum + lifted
            parts.append(lifted.astype(BF16))
        mixed = jnp.dot(jnp.concatenate(parts, axis=1), values[block], preferred_element_type=F32)
        if fresh:
            total_l, acc = part_sum, mixed
        else:
            fade = jnp.exp2((peak - new_peak) * scale)
            total_l = total_l * fade + part_sum
            acc = acc * fade + mixed
        peak = new_peak
        if block == blocks - 1:
            if last:
                (out_ref,) = refs
                whole = jnp.sum(total_l, axis=1, keepdims=True)
                out_ref[here, :] = (acc / whole).astype(BF16)
            else:
                m_out, l_out, acc_out = refs
                m_out[here, :] = peak
                l_out[here, :] = total_l
                acc_out[here, :] = acc


def attend(queries, kv_blocks, state, last, tile=128):
    groups, _, rows, width = queries.shape
    total = groups * rows
    blocks = len(kv_blocks)
    first = state is None
    carried = jax.ShapeDtypeStruct((total, width), F32)
    out_shape = jax.ShapeDtypeStruct((total, width), BF16) if last else (carried,) * 3
    pairs = total * total * blocks
    return pl.pallas_call(
        functools.partial(attend_kernel, first, last, blocks, tile),
        out_shape=out_shape,
        compiler_params=pltpu.CompilerParams(vmem_limit_bytes=16 * 1024 * 1024),
        cost_estimate=pl.CostEstimate(
            flops=pairs * width * 4, bytes_accessed=total * width * 2 * (2 * blocks + 7), transcendentals=pairs
        ),
    )(queries, *kv_blocks, *(() if first else state))


def project_kernel(part, tile, x_ref, w_ref, out_ref):
    x = jnp.concatenate([x_ref[h] for h in range(x_ref.shape[0])], axis=1)
    for c in range(0, out_ref.shape[1], tile):
        mixed = jnp.dot(x, w_ref[part, :, c : c + tile], preferred_element_type=F32)
        out_ref[:, c : c + tile] = mixed.astype(out_ref.dtype)


def project(part, returned, weights, out_type, tile=512):
    heads, tokens, width = returned.shape
    _, rows, columns = weights.shape
    return pl.pallas_call(
        functools.partial(project_kernel, part, tile),
        in_specs=[pl.BlockSpec(memory_space=pltpu.VMEM)] * 2,
        out_specs=pl.BlockSpec(memory_space=pltpu.VMEM),
        out_shape=jax.ShapeDtypeStruct((tokens, columns), out_type),
        compiler_params=pltpu.CompilerParams(vmem_limit_bytes=8 * 1024 * 1024),
        cost_estimate=pl.CostEstimate(
            flops=2 * tokens * rows * columns, bytes_accessed=rows * columns * 2, transcendentals=0
        ),
    )(returned, weights)


HEAD_AXES = ("x", "zl", "yl")
RING = "zh"


def body(head_inputs, positions, code_words, group_scales, out_gate, out_bias):
    ring = lax.axis_size(RING)
    half = lax.axis_index("yh").astype(jnp.int32).reshape(1)
    prepared = rotate(positions, head_inputs)
    grouped = lax.all_to_all(prepared, HEAD_AXES, split_axis=0, concat_axis=0, tiled=True)
    own = grouped[:, 1:]

    def swap(a):
        return lax.ppermute(a, "c", [(0, 1), (1, 0)])

    up = lax.ppermute(own, RING, [(i, (i + 1) % ring) for i in range(ring)])
    down = lax.ppermute(own, RING, [(i, (i - 1) % ring) for i in range(ring)])
    beside = swap(own)
    weights = dequantize(half, code_words, group_scales)
    state = attend(grouped, [grouped, beside], None, False)
    up, down, state, weights = lax.optimization_barrier((up, down, state, weights))
    core = lax.axis_index("c")
    hops = []
    for i in range(ring):
        hops.append((2 * i, 2 * ((i + 1) % ring)))
        hops.append((2 * i + 1, 2 * ((i - 1) % ring) + 1))
    far = lax.ppermute(jnp.where(core == 0, up, down), (RING, "c"), hops)
    up_beside, down_beside = swap(up), swap(down)
    state = attend(grouped, [up, down], state, False)
    state = attend(grouped, [up_beside, down_beside], state, False)
    far, state = lax.optimization_barrier((far, state))
    far_beside = swap(far)
    attended = attend(grouped, [far, far_beside], state, True)
    chunks = prepared.shape[0]
    returned = lax.all_to_all(
        attended.reshape(chunks, -1, HD), HEAD_AXES, split_axis=0, concat_axis=0, tiled=True
    )
    outgoing = project(0, returned, weights, BF16)
    incoming = lax.ppermute(outgoing, "yh", [(0, 1), (1, 0)])
    kept = project(1, returned, weights, F32)
    return out_gate[None, :] * (kept + incoming.astype(F32) + out_bias[None, :])


def solution(mesh):
    x, blk, yh = mesh.devices.shape
    fine = Mesh(mesh.devices.reshape(x, blk // 8, 2, 2, 2, yh), ("x", "zh", "zl", "yl", "c", "yh"))
    tokens = ("x", "zh", "zl", "yl", "c")
    placed = (
        P(tokens, None, "yh", None),
        P(None, tokens),
        P("yh", None),
        P("yh", None),
        P("yh"),
        P("yh"),
    )
    return jax.shard_map(
        body, mesh=fine, in_specs=placed, out_specs=P(tokens, "yh"), check_vma=False
    )
```

```python
import functools
import math

import jax
import jax.numpy as jnp
from jax import lax
from jax.experimental import pallas as pl
from jax.experimental.pallas import tpu as pltpu
from jax.sharding import Mesh
from jax.sharding import PartitionSpec as P

HD = 128
LOG2E = 1.4426950408889634
F32 = jnp.float32
BF16 = jnp.bfloat16


def angle_rates(width):
    frame = (width - 4 * (width // 6)) // 2
    side = width // 6
    pair = lax.broadcasted_iota(jnp.int32, (3, width), 1) // 2
    row = lax.broadcasted_iota(jnp.int32, (3, width), 0)
    start = jnp.where(row == 0, 0, jnp.where(row == 1, frame, frame + side))
    extent = jnp.where(row == 0, frame, side)
    within = pair - start
    rate = jnp.exp(within.astype(F32) / extent.astype(F32) * (-math.log(10000.0)))
    return jnp.where((within >= 0) & (within < extent), rate, 0.0)


def rotate_kernel(pos_hbm, x_hbm, out_ref, pos_ref, x_ref, wide, sems):
    pos_copy = pltpu.make_async_copy(pos_hbm, pos_ref, sems.at[0])
    x_copy = pltpu.make_async_copy(x_hbm, x_ref, sems.at[1])
    pos_copy.start()
    x_copy.start()
    tokens, kinds, heads, width = x_ref.shape
    rates = angle_rates(width)
    is_even = lax.broadcasted_iota(jnp.int32, (tokens, width), 1) % 2 == 0
    pos_copy.wait()
    angles = lax.dot_general(
        pos_ref[...].astype(F32),
        rates,
        (((0,), (0,)), ((), ())),
        precision=lax.Precision.HIGHEST,
        preferred_element_type=F32,
    )
    cosine = jnp.cos(angles)
    sine = jnp.sin(angles)
    sine_even = jnp.where(is_even, -sine, 0.0)
    sine_odd = jnp.where(is_even, 0.0, sine)
    x_copy.wait()
    wide[...] = x_ref[...].astype(F32).reshape(tokens * kinds * heads, width)
    for kind in range(kinds):
        for head in range(heads):
            x = wide[pl.ds(kind * heads + head, tokens, stride=kinds * heads), :]
            if kind < 2:
                right = pltpu.roll(x, 1, 1)
                left = pltpu.roll(x, width - 1, 1)
                x = x * cosine + (left * sine_even + right * sine_odd)
            out_ref[head, kind] = x.astype(BF16)


def rotate(positions, head_inputs):
    tokens, kinds, heads, width = head_inputs.shape
    return pl.pallas_call(
        rotate_kernel,
        in_specs=[pl.BlockSpec(memory_space=pltpu.HBM)] * 2,
        out_specs=pl.BlockSpec(memory_space=pltpu.VMEM),
        out_shape=jax.ShapeDtypeStruct((heads, kinds, tokens, width), BF16),
        scratch_shapes=[
            pltpu.VMEM(positions.shape, positions.dtype),
            pltpu.VMEM(head_inputs.shape, head_inputs.dtype),
            pltpu.VMEM((tokens * kinds * heads, width), F32),
            pltpu.SemaphoreType.DMA((2,)),
        ],
        compiler_params=pltpu.CompilerParams(vmem_limit_bytes=16 * 1024 * 1024),
    )(in_hbm(positions), in_hbm(head_inputs))


def in_hbm(array):
    return pltpu.with_memory_space_constraint(array, pltpu.HBM)


def dequantize_kernel(half_ref, words_ref, scales_ref, out_ref, slots, wide, sems):
    rows, quarter = words_ref.shape
    groups = scales_ref.shape[0]
    depth = rows // groups
    half = half_ref[0]
    ahead, chunk, across = slots.shape[0], 16, 256

    def fetch(g):
        slot = lax.rem(g, ahead)
        start = pl.multiple_of(g * depth, depth)
        return pltpu.make_async_copy(words_ref.at[pl.ds(start, depth)], slots.at[slot], sems.at[slot])

    for g in range(ahead):
        fetch(g).start()
    wide[...] = scales_ref[...].astype(F32)

    def step(g, carry):
        fetch(g).wait()
        slot = lax.rem(g, ahead)
        start = pl.multiple_of(g * depth, depth)
        for column in range(0, quarter, across):
            for part in range(2):
                mine = half if part else 1 - half
                scales = []
                for low in range(2):
                    at = pl.multiple_of((2 * mine + low) * quarter + column, 128)
                    row = wide[pl.ds(g, 1), pl.ds(at, across)] * (0.0625 if low else 1.0)
                    scales.append(jnp.broadcast_to(row, (chunk, across)))
                for r in range(0, depth, chunk):
                    words = slots[slot, r : r + chunk, column : column + across]
                    shifted = lax.shift_right_logical(words, jnp.full(words.shape, 8 * mine, jnp.int32))
                    for low in range(2):
                        level = ((shifted & 240) - 128) if low else ((shifted & 15) - 8)
                        out_ref[
                            part,
                            pl.ds(start + r, chunk),
                            low * quarter + column : low * quarter + column + across,
                        ] = (level.astype(F32) * scales[low]).astype(BF16)

        @pl.when(g + ahead < groups)
        def _():
            fetch(g + ahead).start()

        return carry

    lax.fori_loop(0, groups, step, 0)


def dequantize(half, code_words, group_scales):
    rows, quarter = code_words.shape
    groups = group_scales.shape[0]
    ahead = 4
    return pl.pallas_call(
        dequantize_kernel,
        in_specs=[
            pl.BlockSpec(memory_space=pltpu.SMEM),
            pl.BlockSpec(memory_space=pltpu.HBM),
            pl.BlockSpec(memory_space=pltpu.VMEM),
        ],
        out_specs=pl.BlockSpec(memory_space=pltpu.VMEM),
        out_shape=pltpu.VMEM((2, rows, 2 * quarter), BF16),
        scratch_shapes=[
            pltpu.VMEM((ahead, rows // groups, quarter), jnp.int32),
            pltpu.VMEM(group_scales.shape, F32),
            pltpu.SemaphoreType.DMA((ahead,)),
        ],
        compiler_params=pltpu.CompilerParams(vmem_limit_bytes=8 * 1024 * 1024),
        cost_estimate=pl.CostEstimate(flops=rows * quarter * 30, bytes_accessed=rows * quarter * 12, transcendentals=0),
    )(half, in_hbm(code_words), group_scales)


def attend_kernel(first, last, blocks, after, tile, q_ref, *refs):
    kv_refs = refs[:blocks]
    refs = refs[blocks + after :]
    if not first:
        m_in, l_in, acc_in = refs[:3]
        refs = refs[3:]
    scale = LOG2E / math.sqrt(HD)
    groups, _, rows, width = q_ref.shape
    total = groups * rows
    queries = q_ref[:, 0].reshape(total, width)
    keys, values = [], []
    for ref in kv_refs:
        at = ref.shape[1] - 2
        count = ref.shape[0] * rows
        keys.append(ref[:, at].reshape(count, width))
        values.append(ref[:, at + 1].reshape(count, width))

    def scores(step):
        row, block = divmod(step, blocks)
        return lax.dot_general(
            queries[row * tile : (row + 1) * tile],
            keys[block],
            (((1,), (1,)), ((), ())),
            preferred_element_type=F32,
        )

    steps = (total // tile) * blocks
    ahead = scores(0)
    for step in range(steps):
        row, block = divmod(step, blocks)
        here = slice(row * tile, (row + 1) * tile)
        s = ahead
        if step + 1 < steps:
            ahead = scores(step + 1)
        fresh = first and block == 0
        if block == 0 and not first:
            peak, total_l, acc = m_in[here, :], l_in[here, :], acc_in[here, :]
        s_peak = jnp.broadcast_to(jnp.max(s, axis=1, keepdims=True), (tile, width))
        new_peak = s_peak if fresh else jnp.maximum(peak, s_peak)
        parts, part_sum = [], None
        for lane in range(s.shape[1] // width):
            lifted = jnp.exp2((s[:, lane * width : (lane + 1) * width] - new_peak) * scale)
            part_sum = lifted if part_sum is None else part_sum + lifted
            parts.append(lifted.astype(BF16))
        mixed = jnp.dot(jnp.concatenate(parts, axis=1), values[block], preferred_element_type=F32)
        if fresh:
            total_l, acc = part_sum, mixed
        else:
            fade = jnp.exp2((peak - new_peak) * scale)
            total_l = total_l * fade + part_sum
            acc = acc * fade + mixed
        peak = new_peak
        if block == blocks - 1:
            if last:
                (out_ref,) = refs
                whole = jnp.sum(total_l, axis=1, keepdims=True)
                out_ref[here, :] = (acc / whole).astype(BF16)
            else:
                m_out, l_out, acc_out = refs
                m_out[here, :] = peak
                l_out[here, :] = total_l
                acc_out[here, :] = acc


def attend(queries, kv_blocks, state, last=False, after=(), tile=128):
    groups, _, rows, width = queries.shape
    total = groups * rows
    blocks = len(kv_blocks)
    first = state is None
    carried = jax.ShapeDtypeStruct((total, width), F32)
    out_shape = jax.ShapeDtypeStruct((total, width), BF16) if last else (carried,) * 3
    pairs = total * sum(block.shape[0] * rows for block in kv_blocks)
    return pl.pallas_call(
        functools.partial(attend_kernel, first, last, blocks, len(after), tile),
        out_shape=out_shape,
        compiler_params=pltpu.CompilerParams(vmem_limit_bytes=16 * 1024 * 1024),
        cost_estimate=pl.CostEstimate(
            flops=pairs * width * 4, bytes_accessed=total * width * 2 * (2 * blocks + 7), transcendentals=pairs
        ),
    )(queries, *kv_blocks, *after, *(() if first else state))


def project_kernel(part, tile, x_ref, w_ref, out_ref):
    x = jnp.concatenate([x_ref[h] for h in range(x_ref.shape[0])], axis=1)
    for c in range(0, out_ref.shape[1], tile):
        mixed = jnp.dot(x, w_ref[part, :, c : c + tile], preferred_element_type=F32)
        out_ref[:, c : c + tile] = mixed.astype(out_ref.dtype)


def project(part, returned, weights, out_type, tile=512):
    heads, tokens, width = returned.shape
    _, rows, columns = weights.shape
    return pl.pallas_call(
        functools.partial(project_kernel, part, tile),
        in_specs=[pl.BlockSpec(memory_space=pltpu.VMEM)] * 2,
        out_specs=pl.BlockSpec(memory_space=pltpu.VMEM),
        out_shape=jax.ShapeDtypeStruct((tokens, columns), out_type),
        compiler_params=pltpu.CompilerParams(vmem_limit_bytes=8 * 1024 * 1024),
        cost_estimate=pl.CostEstimate(
            flops=2 * tokens * rows * columns, bytes_accessed=rows * columns * 2, transcendentals=0
        ),
    )(returned, weights)


HEAD_AXES = ("x", "zl", "yl")
RING = "zh"


def body(head_inputs, positions, code_words, group_scales, out_gate, out_bias):
    ring = lax.axis_size(RING)
    half = lax.axis_index("yh").astype(jnp.int32).reshape(1)
    prepared = rotate(positions, head_inputs)
    grouped = lax.all_to_all(prepared, HEAD_AXES, split_axis=0, concat_axis=0, tiled=True)
    own = grouped[:, 1:]

    def swap(a):
        return lax.ppermute(a, "c", [(0, 1), (1, 0)])

    def send(a, way):
        hops = []
        for i in range(ring):
            hops.append((2 * i, 2 * ((i + way) % ring)))
            hops.append((2 * i + 1, 2 * ((i - way) % ring) + 1))
        return lax.ppermute(a, (RING, "c"), hops)

    near = send(own, 1)
    back = send(own, -1)
    beside = swap(own)
    weights = dequantize(half, code_words, group_scales)
    state = attend(grouped, [grouped, beside], None, after=(weights,))
    near, back, state = lax.optimization_barrier((near, back, state))
    far = send(near, 1)
    near_beside = swap(near)
    back_beside = swap(back)
    state = attend(grouped, [near, back], state)
    state = attend(grouped, [near_beside, back_beside], state)
    far, state = lax.optimization_barrier((far, state))
    far_beside = swap(far)
    state = attend(grouped, [far], state)
    attended = attend(grouped, [far_beside], state, True)
    chunks = prepared.shape[0]
    returned = lax.all_to_all(
        attended.reshape(chunks, -1, HD), HEAD_AXES, split_axis=0, concat_axis=0, tiled=True
    )
    outgoing = project(0, returned, weights, BF16)
    incoming = lax.ppermute(outgoing, "yh", [(0, 1), (1, 0)])
    kept = project(1, returned, weights, F32)
    return out_gate[None, :] * (kept + incoming.astype(F32) + out_bias[None, :])


def solution(mesh):
    x, blk, yh = mesh.devices.shape
    fine = Mesh(mesh.devices.reshape(x, blk // 8, 2, 2, 2, yh), ("x", "zh", "zl", "yl", "c", "yh"))
    tokens = ("x", "zh", "zl", "yl", "c")
    placed = (
        P(tokens, None, "yh", None),
        P(None, tokens),
        P("yh", None),
        P("yh", None),
        P("yh"),
        P("yh"),
    )
    return jax.shard_map(
        body, mesh=fine, in_specs=placed, out_specs=P(tokens, "yh"), check_vma=False
    )
```

```python
import functools
import math

import jax
import jax.numpy as jnp
from jax import lax
from jax.experimental import pallas as pl
from jax.experimental.pallas import tpu as pltpu
from jax.sharding import Mesh
from jax.sharding import PartitionSpec as P

HD = 128
LOG2E = 1.4426950408889634
F32 = jnp.float32
BF16 = jnp.bfloat16


def angle_rates(width):
    frame = (width - 4 * (width // 6)) // 2
    side = width // 6
    pair = lax.broadcasted_iota(jnp.int32, (3, width), 1) // 2
    row = lax.broadcasted_iota(jnp.int32, (3, width), 0)
    start = jnp.where(row == 0, 0, jnp.where(row == 1, frame, frame + side))
    extent = jnp.where(row == 0, frame, side)
    within = pair - start
    rate = jnp.exp(within.astype(F32) / extent.astype(F32) * (-math.log(10000.0)))
    return jnp.where((within >= 0) & (within < extent), rate, 0.0)


def rotate_kernel(pos_hbm, x_hbm, out_ref, pos_ref, x_ref, wide, sems):
    pos_copy = pltpu.make_async_copy(pos_hbm, pos_ref, sems.at[0])
    x_copy = pltpu.make_async_copy(x_hbm, x_ref, sems.at[1])
    pos_copy.start()
    x_copy.start()
    tokens, kinds, heads, width = x_ref.shape
    rates = angle_rates(width)
    is_even = lax.broadcasted_iota(jnp.int32, (tokens, width), 1) % 2 == 0
    pos_copy.wait()
    angles = lax.dot_general(
        pos_ref[...].astype(F32),
        rates,
        (((0,), (0,)), ((), ())),
        precision=lax.Precision.HIGHEST,
        preferred_element_type=F32,
    )
    cosine = jnp.cos(angles)
    sine = jnp.sin(angles)
    sine_even = jnp.where(is_even, -sine, 0.0)
    sine_odd = jnp.where(is_even, 0.0, sine)
    x_copy.wait()
    wide[...] = x_ref[...].astype(F32).reshape(tokens * kinds * heads, width)
    for kind in range(kinds):
        for head in range(heads):
            x = wide[pl.ds(kind * heads + head, tokens, stride=kinds * heads), :]
            if kind < 2:
                right = pltpu.roll(x, 1, 1)
                left = pltpu.roll(x, width - 1, 1)
                x = x * cosine + (left * sine_even + right * sine_odd)
            out_ref[head, kind] = x.astype(BF16)


def rotate(positions, head_inputs):
    tokens, kinds, heads, width = head_inputs.shape
    return pl.pallas_call(
        rotate_kernel,
        in_specs=[pl.BlockSpec(memory_space=pltpu.HBM)] * 2,
        out_specs=pl.BlockSpec(memory_space=pltpu.VMEM),
        out_shape=jax.ShapeDtypeStruct((heads, kinds, tokens, width), BF16),
        scratch_shapes=[
            pltpu.VMEM(positions.shape, positions.dtype),
            pltpu.VMEM(head_inputs.shape, head_inputs.dtype),
            pltpu.VMEM((tokens * kinds * heads, width), F32),
            pltpu.SemaphoreType.DMA((2,)),
        ],
        compiler_params=pltpu.CompilerParams(vmem_limit_bytes=16 * 1024 * 1024),
    )(in_hbm(positions), in_hbm(head_inputs))


def in_hbm(array):
    return pltpu.with_memory_space_constraint(array, pltpu.HBM)


def dequantize_kernel(half_ref, words_ref, scales_ref, out_ref, slots, narrow, wide, sems):
    rows, quarter = words_ref.shape
    groups = scales_ref.shape[0]
    depth = rows // groups
    half = half_ref[0]
    ahead, chunk, across = slots.shape[0], 16, 256

    def fetch(g):
        slot = lax.rem(g, ahead)
        start = pl.multiple_of(g * depth, depth)
        return pltpu.make_async_copy(words_ref.at[pl.ds(start, depth)], slots.at[slot], sems.at[slot])

    scales_copy = pltpu.make_async_copy(scales_ref, narrow, sems.at[ahead])
    scales_copy.start()
    for g in range(ahead):
        fetch(g).start()
    scales_copy.wait()
    wide[...] = narrow[...].astype(F32)

    def step(g, carry):
        fetch(g).wait()
        slot = lax.rem(g, ahead)
        start = pl.multiple_of(g * depth, depth)
        for column in range(0, quarter, across):
            for part in range(2):
                mine = half if part else 1 - half
                scales = []
                for low in range(2):
                    at = pl.multiple_of((2 * mine + low) * quarter + column, 128)
                    row = wide[pl.ds(g, 1), pl.ds(at, across)] * (0.0625 if low else 1.0)
                    scales.append(jnp.broadcast_to(row, (chunk, across)).astype(BF16))
                for r in range(0, depth, chunk):
                    words = slots[slot, r : r + chunk, column : column + across]
                    shifted = lax.shift_right_logical(words, jnp.full(words.shape, 8 * mine, jnp.int32))
                    for low in range(2):
                        level = ((shifted & 240) if low else (shifted & 15)).astype(F32).astype(BF16)
                        out_ref[
                            part,
                            pl.ds(start + r, chunk),
                            low * quarter + column : low * quarter + column + across,
                        ] = (level - (128 if low else 8)) * scales[low]

        @pl.when(g + ahead < groups)
        def _():
            fetch(g + ahead).start()

        return carry

    lax.fori_loop(0, groups, step, 0)


def dequantize(half, code_words, group_scales):
    rows, quarter = code_words.shape
    groups = group_scales.shape[0]
    ahead = 4
    return pl.pallas_call(
        dequantize_kernel,
        in_specs=[
            pl.BlockSpec(memory_space=pltpu.SMEM),
            pl.BlockSpec(memory_space=pltpu.HBM),
            pl.BlockSpec(memory_space=pltpu.HBM),
        ],
        out_specs=pl.BlockSpec(memory_space=pltpu.VMEM),
        out_shape=pltpu.VMEM((2, rows, 2 * quarter), BF16),
        scratch_shapes=[
            pltpu.VMEM((ahead, rows // groups, quarter), jnp.int32),
            pltpu.VMEM(group_scales.shape, group_scales.dtype),
            pltpu.VMEM(group_scales.shape, F32),
            pltpu.SemaphoreType.DMA((ahead + 1,)),
        ],
        compiler_params=pltpu.CompilerParams(vmem_limit_bytes=8 * 1024 * 1024),
        cost_estimate=pl.CostEstimate(flops=rows * quarter * 30, bytes_accessed=rows * quarter * 12, transcendentals=0),
    )(half, in_hbm(code_words), in_hbm(group_scales))


def attend_kernel(first, last, blocks, after, tile, q_ref, *refs):
    kv_refs = refs[:blocks]
    refs = refs[blocks + after :]
    if not first:
        m_in, l_in, acc_in = refs[:3]
        refs = refs[3:]
    scale = LOG2E / math.sqrt(HD)
    groups, _, rows, width = q_ref.shape
    total = groups * rows
    queries = q_ref[:, 0].reshape(total, width)
    keys, values = [], []
    for ref in kv_refs:
        at = ref.shape[1] - 2
        count = ref.shape[0] * rows
        keys.append(ref[:, at].reshape(count, width))
        values.append(ref[:, at + 1].reshape(count, width))

    def scores(step):
        row, block = divmod(step, blocks)
        return lax.dot_general(
            queries[row * tile : (row + 1) * tile],
            keys[block],
            (((1,), (1,)), ((), ())),
            preferred_element_type=F32,
        )

    steps = (total // tile) * blocks
    ahead = scores(0)
    for step in range(steps):
        row, block = divmod(step, blocks)
        here = slice(row * tile, (row + 1) * tile)
        s = ahead
        if step + 1 < steps:
            ahead = scores(step + 1)
        fresh = first and block == 0
        if block == 0 and not first:
            peak, total_l, acc = m_in[here, :], l_in[here, :], acc_in[here, :]
        s_peak = jnp.broadcast_to(jnp.max(s, axis=1, keepdims=True), (tile, width))
        new_peak = s_peak if fresh else jnp.maximum(peak, s_peak)
        parts, part_sum = [], None
        for lane in range(s.shape[1] // width):
            lifted = jnp.exp2((s[:, lane * width : (lane + 1) * width] - new_peak) * scale)
            part_sum = lifted if part_sum is None else part_sum + lifted
            parts.append(lifted.astype(BF16))
        mixed = jnp.dot(jnp.concatenate(parts, axis=1), values[block], preferred_element_type=F32)
        if fresh:
            total_l, acc = part_sum, mixed
        else:
            fade = jnp.exp2((peak - new_peak) * scale)
            total_l = total_l * fade + part_sum
            acc = acc * fade + mixed
        peak = new_peak
        if block == blocks - 1:
            if last:
                (out_ref,) = refs
                whole = jnp.sum(total_l, axis=1, keepdims=True)
                out_ref[here, :] = (acc / whole).astype(BF16)
            else:
                m_out, l_out, acc_out = refs
                m_out[here, :] = peak
                l_out[here, :] = total_l
                acc_out[here, :] = acc


def attend(queries, kv_blocks, state, last=False, after=(), tile=128):
    groups, _, rows, width = queries.shape
    total = groups * rows
    blocks = len(kv_blocks)
    first = state is None
    carried = jax.ShapeDtypeStruct((total, width), F32)
    out_shape = jax.ShapeDtypeStruct((total, width), BF16) if last else (carried,) * 3
    pairs = total * sum(block.shape[0] * rows for block in kv_blocks)
    return pl.pallas_call(
        functools.partial(attend_kernel, first, last, blocks, len(after), tile),
        out_shape=out_shape,
        compiler_params=pltpu.CompilerParams(vmem_limit_bytes=16 * 1024 * 1024),
        cost_estimate=pl.CostEstimate(
            flops=pairs * width * 4, bytes_accessed=total * width * 2 * (2 * blocks + 7), transcendentals=pairs
        ),
    )(queries, *kv_blocks, *after, *(() if first else state))


def project_kernel(part, tile, x_ref, w_ref, out_ref):
    x = jnp.concatenate([x_ref[h] for h in range(x_ref.shape[0])], axis=1)
    for c in range(0, out_ref.shape[1], tile):
        mixed = jnp.dot(x, w_ref[part, :, c : c + tile], preferred_element_type=F32)
        out_ref[:, c : c + tile] = mixed.astype(out_ref.dtype)


def project(part, returned, weights, out_type, tile=512):
    heads, tokens, width = returned.shape
    _, rows, columns = weights.shape
    return pl.pallas_call(
        functools.partial(project_kernel, part, tile),
        in_specs=[pl.BlockSpec(memory_space=pltpu.VMEM)] * 2,
        out_specs=pl.BlockSpec(memory_space=pltpu.VMEM),
        out_shape=jax.ShapeDtypeStruct((tokens, columns), out_type),
        compiler_params=pltpu.CompilerParams(vmem_limit_bytes=8 * 1024 * 1024),
        cost_estimate=pl.CostEstimate(
            flops=2 * tokens * rows * columns, bytes_accessed=rows * columns * 2, transcendentals=0
        ),
    )(returned, weights)


HEAD_AXES = ("zh", "zl", "yl")
RING = "x"


def body(head_inputs, positions, code_words, group_scales, out_gate, out_bias):
    ring = lax.axis_size(RING)
    half = lax.axis_index("yh").astype(jnp.int32).reshape(1)
    prepared = rotate(positions, head_inputs)
    grouped = lax.all_to_all(prepared, HEAD_AXES, split_axis=0, concat_axis=0, tiled=True)
    own = grouped[:, 1:]

    def swap(a):
        return lax.ppermute(a, "c", [(0, 1), (1, 0)])

    def send(a, way):
        hops = []
        for i in range(ring):
            hops.append((2 * i, 2 * ((i + way) % ring)))
            hops.append((2 * i + 1, 2 * ((i - way) % ring) + 1))
        return lax.ppermute(a, (RING, "c"), hops)

    near = send(own, 1)
    back = send(own, -1)
    weights = dequantize(half, code_words, group_scales)
    near, back, own, weights = lax.optimization_barrier((near, back, own, weights))
    far = send(near, 1)
    beside, near_beside, back_beside = swap(own), swap(near), swap(back)
    state = attend(grouped, [own, near, back], None)
    state = attend(grouped, [beside, near_beside, back_beside], state)
    far, state = lax.optimization_barrier((far, state))
    far_beside = swap(far)
    state = attend(grouped, [far], state)
    attended = attend(grouped, [far_beside], state, True)
    chunks = prepared.shape[0]
    returned = lax.all_to_all(
        attended.reshape(chunks, -1, HD), HEAD_AXES, split_axis=0, concat_axis=0, tiled=True
    )
    outgoing = project(0, returned, weights, BF16)
    incoming = lax.ppermute(outgoing, "yh", [(0, 1), (1, 0)])
    kept = project(1, returned, weights, F32)
    return out_gate[None, :] * (kept + incoming.astype(F32) + out_bias[None, :])


def solution(mesh):
    x, blk, yh = mesh.devices.shape
    fine = Mesh(mesh.devices.reshape(x, blk // 8, 2, 2, 2, yh), ("x", "zh", "zl", "yl", "c", "yh"))
    tokens = ("x", "zh", "zl", "yl", "c")
    placed = (
        P(tokens, None, "yh", None),
        P(None, tokens),
        P("yh", None),
        P("yh", None),
        P("yh"),
        P("yh"),
    )
    return jax.shard_map(
        body, mesh=fine, in_specs=placed, out_specs=P(tokens, "yh"), check_vma=False
    )
```

```python
import functools
import math

import jax
import jax.numpy as jnp
from jax import lax
from jax.experimental import pallas as pl
from jax.experimental.pallas import tpu as pltpu
from jax.sharding import Mesh
from jax.sharding import PartitionSpec as P

HD = 128
LOG2E = 1.4426950408889634
F32 = jnp.float32
BF16 = jnp.bfloat16


def angle_rates(width):
    frame = (width - 4 * (width // 6)) // 2
    side = width // 6
    pair = lax.broadcasted_iota(jnp.int32, (3, width), 1) // 2
    row = lax.broadcasted_iota(jnp.int32, (3, width), 0)
    start = jnp.where(row == 0, 0, jnp.where(row == 1, frame, frame + side))
    extent = jnp.where(row == 0, frame, side)
    within = pair - start
    rate = jnp.exp(within.astype(F32) / extent.astype(F32) * (-math.log(10000.0)))
    return jnp.where((within >= 0) & (within < extent), rate, 0.0)


def rotate_kernel(pos_hbm, x_hbm, q_ref, kv_ref, pos_ref, x_ref, wide, sems):
    pos_copy = pltpu.make_async_copy(pos_hbm, pos_ref, sems.at[0])
    x_copy = pltpu.make_async_copy(x_hbm, x_ref, sems.at[1])
    pos_copy.start()
    x_copy.start()
    tokens, kinds, heads, width = x_ref.shape
    rates = angle_rates(width)
    is_even = lax.broadcasted_iota(jnp.int32, (tokens, width), 1) % 2 == 0
    pos_copy.wait()
    angles = lax.dot_general(
        pos_ref[...].astype(F32),
        rates,
        (((0,), (0,)), ((), ())),
        precision=lax.Precision.HIGHEST,
        preferred_element_type=F32,
    )
    cosine = jnp.cos(angles)
    sine = jnp.sin(angles)
    sine_even = jnp.where(is_even, -sine, 0.0)
    sine_odd = jnp.where(is_even, 0.0, sine)
    x_copy.wait()
    wide[...] = x_ref[...].astype(F32).reshape(tokens * kinds * heads, width)
    for kind in range(kinds):
        for head in range(heads):
            x = wide[pl.ds(kind * heads + head, tokens, stride=kinds * heads), :]
            if kind < 2:
                right = pltpu.roll(x, 1, 1)
                left = pltpu.roll(x, width - 1, 1)
                x = x * cosine + (left * sine_even + right * sine_odd)
            if kind:
                kv_ref[head, kind - 1] = x.astype(BF16)
            else:
                q_ref[head] = x.astype(BF16)


def rotate(positions, head_inputs):
    tokens, kinds, heads, width = head_inputs.shape
    return pl.pallas_call(
        rotate_kernel,
        in_specs=[pl.BlockSpec(memory_space=pltpu.HBM)] * 2,
        out_specs=[pl.BlockSpec(memory_space=pltpu.VMEM)] * 2,
        out_shape=[
            jax.ShapeDtypeStruct((heads, tokens, width), BF16),
            jax.ShapeDtypeStruct((heads, kinds - 1, tokens, width), BF16),
        ],
        scratch_shapes=[
            pltpu.VMEM(positions.shape, positions.dtype),
            pltpu.VMEM(head_inputs.shape, head_inputs.dtype),
            pltpu.VMEM((tokens * kinds * heads, width), F32),
            pltpu.SemaphoreType.DMA((2,)),
        ],
        compiler_params=pltpu.CompilerParams(vmem_limit_bytes=16 * 1024 * 1024),
    )(in_hbm(positions), in_hbm(head_inputs))


def in_hbm(array):
    return pltpu.with_memory_space_constraint(array, pltpu.HBM)


def dequantize_kernel(half_ref, words_ref, scales_ref, out_ref, slots, narrow, wide, sems):
    rows, quarter = words_ref.shape
    groups = scales_ref.shape[0]
    depth = rows // groups
    half = half_ref[0]
    ahead, chunk, across = slots.shape[0], 16, 256

    def fetch(g):
        slot = lax.rem(g, ahead)
        start = pl.multiple_of(g * depth, depth)
        return pltpu.make_async_copy(words_ref.at[pl.ds(start, depth)], slots.at[slot], sems.at[slot])

    scales_copy = pltpu.make_async_copy(scales_ref, narrow, sems.at[ahead])
    scales_copy.start()
    for g in range(ahead):
        fetch(g).start()
    scales_copy.wait()
    wide[...] = narrow[...].astype(F32)

    def step(g, carry):
        fetch(g).wait()
        slot = lax.rem(g, ahead)
        start = pl.multiple_of(g * depth, depth)
        for column in range(0, quarter, across):
            scales = []
            for low in range(2):
                at = pl.multiple_of((2 * half + low) * quarter + column, 128)
                row = wide[pl.ds(g, 1), pl.ds(at, across)] * (0.0625 if low else 1.0)
                scales.append(jnp.broadcast_to(row, (chunk, across)).astype(BF16))
            for r in range(0, depth, chunk):
                words = slots[slot, r : r + chunk, column : column + across]
                shifted = lax.shift_right_logical(words, jnp.full(words.shape, 8 * half, jnp.int32))
                for low in range(2):
                    level = ((shifted & 240) if low else (shifted & 15)).astype(F32).astype(BF16)
                    out_ref[
                        pl.ds(start + r, chunk),
                        low * quarter + column : low * quarter + column + across,
                    ] = (level - (128 if low else 8)) * scales[low]

        @pl.when(g + ahead < groups)
        def _():
            fetch(g + ahead).start()

        return carry

    lax.fori_loop(0, groups, step, 0)


def dequantize(half, code_words, group_scales):
    rows, quarter = code_words.shape
    groups = group_scales.shape[0]
    ahead = 8
    return pl.pallas_call(
        dequantize_kernel,
        in_specs=[
            pl.BlockSpec(memory_space=pltpu.SMEM),
            pl.BlockSpec(memory_space=pltpu.HBM),
            pl.BlockSpec(memory_space=pltpu.HBM),
        ],
        out_specs=pl.BlockSpec(memory_space=pltpu.VMEM),
        out_shape=pltpu.VMEM((rows, 2 * quarter), BF16),
        scratch_shapes=[
            pltpu.VMEM((ahead, rows // groups, quarter), jnp.int32),
            pltpu.VMEM(group_scales.shape, group_scales.dtype),
            pltpu.VMEM(group_scales.shape, F32),
            pltpu.SemaphoreType.DMA((ahead + 1,)),
        ],
        compiler_params=pltpu.CompilerParams(vmem_limit_bytes=12 * 1024 * 1024),
        cost_estimate=pl.CostEstimate(flops=rows * quarter * 15, bytes_accessed=rows * quarter * 8, transcendentals=0),
    )(half, in_hbm(code_words), in_hbm(group_scales))


def attend_kernel(first, last, blocks, after, tile, q_ref, *refs):
    kv_refs = refs[:blocks]
    refs = refs[blocks + after :]
    if not first:
        m_in, l_in, acc_in = refs[:3]
        refs = refs[3:]
    scale = LOG2E / math.sqrt(HD)
    groups, rows, width = q_ref.shape
    total = groups * rows
    queries = q_ref[...].reshape(total, width)
    keys, values = [], []
    for ref in kv_refs:
        count = ref.shape[0] * rows
        keys.append(ref[:, 0].reshape(count, width))
        values.append(ref[:, 1].reshape(count, width))

    def scores(step):
        row, block = divmod(step, blocks)
        return lax.dot_general(
            queries[row * tile : (row + 1) * tile],
            keys[block],
            (((1,), (1,)), ((), ())),
            preferred_element_type=F32,
        )

    steps = (total // tile) * blocks
    ahead = scores(0)
    for step in range(steps):
        row, block = divmod(step, blocks)
        here = slice(row * tile, (row + 1) * tile)
        s = ahead
        if step + 1 < steps:
            ahead = scores(step + 1)
        fresh = first and block == 0
        if block == 0 and not first:
            peak, total_l, acc = m_in[here, :], l_in[here, :], acc_in[here, :]
        s_peak = jnp.broadcast_to(jnp.max(s, axis=1, keepdims=True), (tile, width))
        new_peak = s_peak if fresh else jnp.maximum(peak, s_peak)
        parts, part_sum = [], None
        for lane in range(s.shape[1] // width):
            lifted = jnp.exp2((s[:, lane * width : (lane + 1) * width] - new_peak) * scale)
            part_sum = lifted if part_sum is None else part_sum + lifted
            parts.append(lifted.astype(BF16))
        mixed = jnp.dot(jnp.concatenate(parts, axis=1), values[block], preferred_element_type=F32)
        if fresh:
            total_l, acc = part_sum, mixed
        else:
            fade = jnp.exp2((peak - new_peak) * scale)
            total_l = total_l * fade + part_sum
            acc = acc * fade + mixed
        peak = new_peak
        if block == blocks - 1:
            if last:
                (out_ref,) = refs
                whole = jnp.sum(total_l, axis=1, keepdims=True)
                out_ref[here, :] = (acc / whole).astype(BF16)
            else:
                m_out, l_out, acc_out = refs
                m_out[here, :] = peak
                l_out[here, :] = total_l
                acc_out[here, :] = acc


def attend(queries, kv_blocks, state, last=False, after=(), tile=384):
    groups, rows, width = queries.shape
    total = groups * rows
    blocks = len(kv_blocks)
    first = state is None
    carried = jax.ShapeDtypeStruct((total, width), F32)
    out_shape = jax.ShapeDtypeStruct((total, width), BF16) if last else (carried,) * 3
    pairs = total * sum(block.shape[0] * rows for block in kv_blocks)
    return pl.pallas_call(
        functools.partial(attend_kernel, first, last, blocks, len(after), tile),
        out_shape=out_shape,
        compiler_params=pltpu.CompilerParams(vmem_limit_bytes=16 * 1024 * 1024),
        cost_estimate=pl.CostEstimate(
            flops=pairs * width * 4, bytes_accessed=total * width * 2 * (2 * blocks + 7), transcendentals=pairs
        ),
    )(queries, *kv_blocks, *after, *(() if first else state))


def project_kernel(tile, x_ref, w_ref, out_ref):
    x = jnp.concatenate([x_ref[h] for h in range(x_ref.shape[0])], axis=1)
    for c in range(0, out_ref.shape[1], tile):
        mixed = jnp.dot(x, w_ref[:, c : c + tile], preferred_element_type=F32)
        out_ref[:, c : c + tile] = mixed.astype(out_ref.dtype)


def project(returned, weights, out_type, tile=512):
    heads, tokens, width = returned.shape
    rows, columns = weights.shape
    return pl.pallas_call(
        functools.partial(project_kernel, tile),
        in_specs=[pl.BlockSpec(memory_space=pltpu.VMEM)] * 2,
        out_specs=pl.BlockSpec(memory_space=pltpu.VMEM),
        out_shape=jax.ShapeDtypeStruct((tokens, columns), out_type),
        compiler_params=pltpu.CompilerParams(vmem_limit_bytes=8 * 1024 * 1024),
        cost_estimate=pl.CostEstimate(
            flops=2 * tokens * rows * columns, bytes_accessed=rows * columns * 2, transcendentals=0
        ),
    )(returned, weights)


HEAD_AXES = ("zh", "zl", "yl")
RING = "x"


def body(head_inputs, positions, code_words, group_scales, out_gate, out_bias):
    ring = lax.axis_size(RING)
    half = lax.axis_index("yh").astype(jnp.int32).reshape(1)
    turned_queries, turned_pairs = rotate(positions, head_inputs)

    def regroup(a):
        return lax.all_to_all(a, HEAD_AXES, split_axis=0, concat_axis=0, tiled=True)

    def swap(a):
        return lax.ppermute(a, "c", [(0, 1), (1, 0)])

    def send(a, way):
        hops = []
        for i in range(ring):
            hops.append((2 * i, 2 * ((i + way) % ring)))
            hops.append((2 * i + 1, 2 * ((i - way) % ring) + 1))
        return lax.ppermute(a, (RING, "c"), hops)

    own = regroup(turned_pairs)
    theirs = dequantize(1 - half, code_words, group_scales)
    own, theirs, turned_queries = lax.optimization_barrier((own, theirs, turned_queries))
    near = send(own, 1)
    back = send(own, -1)
    queries = regroup(turned_queries)
    near, back, own = lax.optimization_barrier((near, back, own))
    far = send(near, 1)
    beside, near_beside, back_beside = swap(own), swap(near), swap(back)
    state = attend(queries, [own, near, back], None)
    state = attend(queries, [beside, near_beside, back_beside], state)
    far, state = lax.optimization_barrier((far, state))
    far_beside = swap(far)
    state = attend(queries, [far], state)
    attended = attend(queries, [far_beside], state, True)
    returned = regroup(attended.reshape(queries.shape))
    returned, half = lax.optimization_barrier((returned, half))
    mine = dequantize(half, code_words, group_scales)
    outgoing = project(returned, theirs, BF16)
    incoming = lax.ppermute(outgoing, "yh", [(0, 1), (1, 0)])
    kept = project(returned, mine, F32)
    return out_gate[None, :] * (kept + incoming.astype(F32) + out_bias[None, :])


def solution(mesh):
    x, blk, yh = mesh.devices.shape
    fine = Mesh(mesh.devices.reshape(x, blk // 8, 2, 2, 2, yh), ("x", "zh", "zl", "yl", "c", "yh"))
    tokens = ("x", "zh", "zl", "yl", "c")
    placed = (
        P(tokens, None, "yh", None),
        P(None, tokens),
        P("yh", None),
        P("yh", None),
        P("yh"),
        P("yh"),
    )
    return jax.shard_map(
        body, mesh=fine, in_specs=placed, out_specs=P(tokens, "yh"), check_vma=False
    )
```

```python
import functools
import math

import jax
import jax.numpy as jnp
from jax import lax
from jax.experimental import pallas as pl
from jax.experimental.pallas import tpu as pltpu
from jax.sharding import Mesh
from jax.sharding import PartitionSpec as P

HD = 128
LOG2E = 1.4426950408889634
F32 = jnp.float32
BF16 = jnp.bfloat16


def angle_rates(width):
    frame = (width - 4 * (width // 6)) // 2
    side = width // 6
    pair = lax.broadcasted_iota(jnp.int32, (3, width), 1) // 2
    row = lax.broadcasted_iota(jnp.int32, (3, width), 0)
    start = jnp.where(row == 0, 0, jnp.where(row == 1, frame, frame + side))
    extent = jnp.where(row == 0, frame, side)
    within = pair - start
    rate = jnp.exp(within.astype(F32) / extent.astype(F32) * (-math.log(10000.0)))
    return jnp.where((within >= 0) & (within < extent), rate, 0.0)


def rotate_kernel(pos_hbm, x_hbm, q_ref, kv_ref, pos_ref, x_ref, wide, sems):
    pos_copy = pltpu.make_async_copy(pos_hbm, pos_ref, sems.at[0])
    x_copy = pltpu.make_async_copy(x_hbm, x_ref, sems.at[1])
    pos_copy.start()
    x_copy.start()
    tokens, kinds, heads, width = x_ref.shape
    rates = angle_rates(width)
    is_even = lax.broadcasted_iota(jnp.int32, (tokens, width), 1) % 2 == 0
    pos_copy.wait()
    angles = lax.dot_general(
        pos_ref[...].astype(F32),
        rates,
        (((0,), (0,)), ((), ())),
        precision=lax.Precision.HIGHEST,
        preferred_element_type=F32,
    )
    cosine = jnp.cos(angles)
    sine = jnp.sin(angles)
    sine_even = jnp.where(is_even, -sine, 0.0)
    sine_odd = jnp.where(is_even, 0.0, sine)
    x_copy.wait()
    wide[...] = x_ref[...].astype(F32).reshape(tokens * kinds * heads, width)
    for kind in range(kinds):
        for head in range(heads):
            x = wide[pl.ds(kind * heads + head, tokens, stride=kinds * heads), :]
            if kind < 2:
                right = pltpu.roll(x, 1, 1)
                left = pltpu.roll(x, width - 1, 1)
                x = x * cosine + (left * sine_even + right * sine_odd)
            if kind:
                kv_ref[head, kind - 1] = x.astype(BF16)
            else:
                q_ref[head] = x.astype(BF16)


def rotate(positions, head_inputs):
    tokens, kinds, heads, width = head_inputs.shape
    return pl.pallas_call(
        rotate_kernel,
        in_specs=[pl.BlockSpec(memory_space=pltpu.HBM)] * 2,
        out_specs=[pl.BlockSpec(memory_space=pltpu.VMEM)] * 2,
        out_shape=[
            jax.ShapeDtypeStruct((heads, tokens, width), BF16),
            jax.ShapeDtypeStruct((heads, kinds - 1, tokens, width), BF16),
        ],
        scratch_shapes=[
            pltpu.VMEM(positions.shape, positions.dtype),
            pltpu.VMEM(head_inputs.shape, head_inputs.dtype),
            pltpu.VMEM((tokens * kinds * heads, width), F32),
            pltpu.SemaphoreType.DMA((2,)),
        ],
        compiler_params=pltpu.CompilerParams(vmem_limit_bytes=16 * 1024 * 1024),
    )(in_hbm(positions), in_hbm(head_inputs))


def in_hbm(array):
    return pltpu.with_memory_space_constraint(array, pltpu.HBM)


def dequantize_kernel(half_ref, words_ref, scales_ref, out_ref, slots, narrow, wide, sems):
    rows, quarter = words_ref.shape
    groups = scales_ref.shape[0]
    depth = rows // groups
    half = half_ref[0]
    ahead, chunk, across = slots.shape[0], 16, 256

    def fetch(g):
        slot = lax.rem(g, ahead)
        start = pl.multiple_of(g * depth, depth)
        return pltpu.make_async_copy(words_ref.at[pl.ds(start, depth)], slots.at[slot], sems.at[slot])

    scales_copy = pltpu.make_async_copy(scales_ref, narrow, sems.at[ahead])
    scales_copy.start()
    for g in range(ahead):
        fetch(g).start()
    scales_copy.wait()
    wide[...] = narrow[...].astype(F32)

    upper = half == 1
    block = (chunk, across)
    masks = [jnp.full(block, jnp.where(upper, 3840 << (4 * low), 15 << (4 * low)), jnp.int32) for low in range(2)]
    middles = [
        jnp.full(block, jnp.where(upper, 2048.0 * 16**low, 8.0 * 16**low), F32).astype(BF16) for low in range(2)
    ]
    shrink = [jnp.where(upper, 0.00390625 / 16**low, 1.0 / 16**low) for low in range(2)]

    def step(g, carry):
        fetch(g).wait()
        slot = lax.rem(g, ahead)
        start = pl.multiple_of(g * depth, depth)
        for column in range(0, quarter, across):
            scales = []
            for low in range(2):
                at = pl.multiple_of((2 * half + low) * quarter + column, 128)
                row = wide[pl.ds(g, 1), pl.ds(at, across)] * shrink[low]
                scales.append(jnp.broadcast_to(row, (chunk, across)).astype(BF16))
            for r in range(0, depth, chunk):
                words = slots[slot, r : r + chunk, column : column + across]
                for low in range(2):
                    level = (words & masks[low]).astype(F32).astype(BF16)
                    out_ref[
                        pl.ds(start + r, chunk),
                        low * quarter + column : low * quarter + column + across,
                    ] = (level - middles[low]) * scales[low]

        @pl.when(g + ahead < groups)
        def _():
            fetch(g + ahead).start()

        return carry

    lax.fori_loop(0, groups, step, 0)


def dequantize(half, code_words, group_scales):
    rows, quarter = code_words.shape
    groups = group_scales.shape[0]
    ahead = 8
    return pl.pallas_call(
        dequantize_kernel,
        in_specs=[
            pl.BlockSpec(memory_space=pltpu.SMEM),
            pl.BlockSpec(memory_space=pltpu.HBM),
            pl.BlockSpec(memory_space=pltpu.HBM),
        ],
        out_specs=pl.BlockSpec(memory_space=pltpu.VMEM),
        out_shape=pltpu.VMEM((rows, 2 * quarter), BF16),
        scratch_shapes=[
            pltpu.VMEM((ahead, rows // groups, quarter), jnp.int32),
            pltpu.VMEM(group_scales.shape, group_scales.dtype),
            pltpu.VMEM(group_scales.shape, F32),
            pltpu.SemaphoreType.DMA((ahead + 1,)),
        ],
        compiler_params=pltpu.CompilerParams(vmem_limit_bytes=12 * 1024 * 1024),
        cost_estimate=pl.CostEstimate(flops=rows * quarter * 15, bytes_accessed=rows * quarter * 8, transcendentals=0),
    )(half, in_hbm(code_words), in_hbm(group_scales))


def attend_kernel(first, last, blocks, after, tile, q_ref, *refs):
    kv_refs = refs[:blocks]
    refs = refs[blocks + after :]
    if not first:
        m_in, l_in, acc_in = refs[:3]
        refs = refs[3:]
    scale = LOG2E / math.sqrt(HD)
    groups, rows, width = q_ref.shape
    total = groups * rows
    queries = q_ref[...].reshape(total, width)
    keys, values = [], []
    for ref in kv_refs:
        count = ref.shape[0] * rows
        keys.append(ref[:, 0].reshape(count, width))
        values.append(ref[:, 1].reshape(count, width))

    def scores(step):
        row, block = divmod(step, blocks)
        return lax.dot_general(
            queries[row * tile : (row + 1) * tile],
            keys[block],
            (((1,), (1,)), ((), ())),
            preferred_element_type=F32,
        )

    steps = (total // tile) * blocks
    ahead = scores(0)
    for step in range(steps):
        row, block = divmod(step, blocks)
        here = slice(row * tile, (row + 1) * tile)
        s = ahead
        if step + 1 < steps:
            ahead = scores(step + 1)
        fresh = first and block == 0
        if block == 0 and not first:
            peak, total_l, acc = m_in[here, :], l_in[here, :], acc_in[here, :]
        s_peak = jnp.broadcast_to(jnp.max(s, axis=1, keepdims=True), (tile, width))
        new_peak = s_peak if fresh else jnp.maximum(peak, s_peak)
        parts, part_sum = [], None
        for lane in range(s.shape[1] // width):
            lifted = jnp.exp2((s[:, lane * width : (lane + 1) * width] - new_peak) * scale)
            part_sum = lifted if part_sum is None else part_sum + lifted
            parts.append(lifted.astype(BF16))
        mixed = jnp.dot(jnp.concatenate(parts, axis=1), values[block], preferred_element_type=F32)
        if fresh:
            total_l, acc = part_sum, mixed
        else:
            fade = jnp.exp2((peak - new_peak) * scale)
            total_l = total_l * fade + part_sum
            acc = acc * fade + mixed
        peak = new_peak
        if block == blocks - 1:
            if last:
                (out_ref,) = refs
                whole = jnp.sum(total_l, axis=1, keepdims=True)
                out_ref[here, :] = (acc / whole).astype(BF16)
            else:
                m_out, l_out, acc_out = refs
                m_out[here, :] = peak
                l_out[here, :] = total_l
                acc_out[here, :] = acc


def attend(queries, kv_blocks, state, last=False, after=(), tile=384):
    groups, rows, width = queries.shape
    total = groups * rows
    blocks = len(kv_blocks)
    first = state is None
    carried = jax.ShapeDtypeStruct((total, width), F32)
    out_shape = jax.ShapeDtypeStruct((total, width), BF16) if last else (carried,) * 3
    pairs = total * sum(block.shape[0] * rows for block in kv_blocks)
    return pl.pallas_call(
        functools.partial(attend_kernel, first, last, blocks, len(after), tile),
        out_shape=out_shape,
        compiler_params=pltpu.CompilerParams(vmem_limit_bytes=16 * 1024 * 1024),
        cost_estimate=pl.CostEstimate(
            flops=pairs * width * 4, bytes_accessed=total * width * 2 * (2 * blocks + 7), transcendentals=pairs
        ),
    )(queries, *kv_blocks, *after, *(() if first else state))


def project_kernel(tile, x_ref, w_ref, out_ref):
    x = jnp.concatenate([x_ref[h] for h in range(x_ref.shape[0])], axis=1)
    for c in range(0, out_ref.shape[1], tile):
        mixed = jnp.dot(x, w_ref[:, c : c + tile], preferred_element_type=F32)
        out_ref[:, c : c + tile] = mixed.astype(out_ref.dtype)


def project(returned, weights, out_type, tile=512):
    heads, tokens, width = returned.shape
    rows, columns = weights.shape
    return pl.pallas_call(
        functools.partial(project_kernel, tile),
        in_specs=[pl.BlockSpec(memory_space=pltpu.VMEM)] * 2,
        out_specs=pl.BlockSpec(memory_space=pltpu.VMEM),
        out_shape=jax.ShapeDtypeStruct((tokens, columns), out_type),
        compiler_params=pltpu.CompilerParams(vmem_limit_bytes=8 * 1024 * 1024),
        cost_estimate=pl.CostEstimate(
            flops=2 * tokens * rows * columns, bytes_accessed=rows * columns * 2, transcendentals=0
        ),
    )(returned, weights)


HEAD_AXES = ("zh", "zl", "yl")
RING = "x"


def body(head_inputs, positions, code_words, group_scales, out_gate, out_bias):
    ring = lax.axis_size(RING)
    half = lax.axis_index("yh").astype(jnp.int32).reshape(1)
    turned_queries, turned_pairs = rotate(positions, head_inputs)

    def regroup(a):
        return lax.all_to_all(a, HEAD_AXES, split_axis=0, concat_axis=0, tiled=True)

    def swap(a):
        return lax.ppermute(a, "c", [(0, 1), (1, 0)])

    def send(a, way):
        hops = []
        for i in range(ring):
            hops.append((2 * i, 2 * ((i + way) % ring)))
            hops.append((2 * i + 1, 2 * ((i - way) % ring) + 1))
        return lax.ppermute(a, (RING, "c"), hops)

    own = regroup(turned_pairs)
    theirs = dequantize(1 - half, code_words, group_scales)
    own, theirs, turned_queries = lax.optimization_barrier((own, theirs, turned_queries))
    near = send(own, 1)
    back = send(own, -1)
    queries = regroup(turned_queries)
    near, back, own = lax.optimization_barrier((near, back, own))
    far = send(back, -1)
    beside, near_beside, back_beside = swap(own), swap(near), swap(back)
    state = attend(queries, [own, near, back], None)
    state = attend(queries, [beside, near_beside, back_beside], state)
    far, state = lax.optimization_barrier((far, state))
    far_beside = swap(far)
    state = attend(queries, [far], state)
    attended = attend(queries, [far_beside], state, True)
    returned = regroup(attended.reshape(queries.shape))
    returned, half = lax.optimization_barrier((returned, half))
    mine = dequantize(half, code_words, group_scales)
    outgoing = project(returned, theirs, BF16)
    incoming = lax.ppermute(outgoing, "yh", [(0, 1), (1, 0)])
    kept = project(returned, mine, F32)
    return out_gate[None, :] * (kept + incoming.astype(F32) + out_bias[None, :])


def solution(mesh):
    x, blk, yh = mesh.devices.shape
    fine = Mesh(mesh.devices.reshape(x, blk // 8, 2, 2, 2, yh), ("x", "zh", "zl", "yl", "c", "yh"))
    tokens = ("x", "zh", "zl", "yl", "c")
    placed = (
        P(tokens, None, "yh", None),
        P(None, tokens),
        P("yh", None),
        P("yh", None),
        P("yh"),
        P("yh"),
    )
    return jax.shard_map(
        body, mesh=fine, in_specs=placed, out_specs=P(tokens, "yh"), check_vma=False
    )
```

```python
import functools
import math

import jax
import jax.numpy as jnp
from jax import lax
from jax.experimental import pallas as pl
from jax.experimental.pallas import tpu as pltpu
from jax.sharding import Mesh
from jax.sharding import PartitionSpec as P

HD = 128
LOG2E = 1.4426950408889634
F32 = jnp.float32
BF16 = jnp.bfloat16


def angle_rates(width):
    frame = (width - 4 * (width // 6)) // 2
    side = width // 6
    pair = lax.broadcasted_iota(jnp.int32, (3, width), 1) // 2
    row = lax.broadcasted_iota(jnp.int32, (3, width), 0)
    start = jnp.where(row == 0, 0, jnp.where(row == 1, frame, frame + side))
    extent = jnp.where(row == 0, frame, side)
    within = pair - start
    rate = jnp.exp(within.astype(F32) / extent.astype(F32) * (-math.log(10000.0)))
    return jnp.where((within >= 0) & (within < extent), rate, 0.0)


def rotate_kernel(pos_hbm, x_hbm, q_ref, kv_ref, pos_ref, x_ref, wide, sems):
    pos_copy = pltpu.make_async_copy(pos_hbm, pos_ref, sems.at[0])
    x_copy = pltpu.make_async_copy(x_hbm, x_ref, sems.at[1])
    pos_copy.start()
    x_copy.start()
    tokens, kinds, heads, width = x_ref.shape
    rates = angle_rates(width)
    is_even = lax.broadcasted_iota(jnp.int32, (tokens, width), 1) % 2 == 0
    pos_copy.wait()
    angles = lax.dot_general(
        pos_ref[...].astype(F32),
        rates,
        (((0,), (0,)), ((), ())),
        precision=lax.Precision.HIGHEST,
        preferred_element_type=F32,
    )
    cosine = jnp.cos(angles)
    sine = jnp.sin(angles)
    sine_even = jnp.where(is_even, -sine, 0.0)
    sine_odd = jnp.where(is_even, 0.0, sine)
    x_copy.wait()
    wide[: tokens * kinds * heads, :] = x_ref[...].astype(F32).reshape(tokens * kinds * heads, width)
    for kind in range(kinds):
        for head in range(heads):
            x = wide[pl.ds(kind * heads + head, tokens, stride=kinds * heads), :]
            if kind < 2:
                right = pltpu.roll(x, 1, 1)
                left = pltpu.roll(x, width - 1, 1)
                x = x * cosine + (left * sine_even + right * sine_odd)
            if kind:
                kv_ref[head, kind - 1] = x.astype(BF16)
            else:
                q_ref[head] = x.astype(BF16)


def rotate(positions, head_inputs):
    tokens, kinds, heads, width = head_inputs.shape
    return pl.pallas_call(
        rotate_kernel,
        in_specs=[pl.BlockSpec(memory_space=pltpu.HBM)] * 2,
        out_specs=[pl.BlockSpec(memory_space=pltpu.VMEM)] * 2,
        out_shape=[
            jax.ShapeDtypeStruct((heads, tokens, width), BF16),
            jax.ShapeDtypeStruct((heads, kinds - 1, tokens, width), BF16),
        ],
        scratch_shapes=[
            pltpu.VMEM(positions.shape, positions.dtype),
            pltpu.VMEM(head_inputs.shape, head_inputs.dtype),
            pltpu.VMEM(((tokens + 1) * kinds * heads, width), F32),
            pltpu.SemaphoreType.DMA((2,)),
        ],
        compiler_params=pltpu.CompilerParams(vmem_limit_bytes=16 * 1024 * 1024),
    )(in_hbm(positions), in_hbm(head_inputs))


def in_hbm(array):
    return pltpu.with_memory_space_constraint(array, pltpu.HBM)


def dequantize_kernel(half_ref, words_ref, scales_ref, out_ref, slots, narrow, wide, sems):
    rows, quarter = words_ref.shape
    groups = scales_ref.shape[0]
    depth = rows // groups
    half = half_ref[0]
    ahead, chunk, across = slots.shape[0], 16, 256

    def fetch(g):
        slot = lax.rem(g, ahead)
        start = pl.multiple_of(g * depth, depth)
        return pltpu.make_async_copy(words_ref.at[pl.ds(start, depth)], slots.at[slot], sems.at[slot])

    scales_copy = pltpu.make_async_copy(scales_ref, narrow, sems.at[ahead])
    scales_copy.start()
    for g in range(ahead):
        fetch(g).start()
    scales_copy.wait()
    wide[...] = narrow[...].astype(F32)

    upper = half == 1
    block = (chunk, across)
    masks = [jnp.full(block, jnp.where(upper, 3840 << (4 * low), 15 << (4 * low)), jnp.int32) for low in range(2)]
    middles = [
        jnp.full(block, jnp.where(upper, 2048.0 * 16**low, 8.0 * 16**low), F32).astype(BF16) for low in range(2)
    ]
    shrink = [jnp.where(upper, 0.00390625 / 16**low, 1.0 / 16**low) for low in range(2)]

    def step(g, carry):
        fetch(g).wait()
        slot = lax.rem(g, ahead)
        start = pl.multiple_of(g * depth, depth)
        for column in range(0, quarter, across):
            scales = []
            for low in range(2):
                at = pl.multiple_of((2 * half + low) * quarter + column, 128)
                row = wide[pl.ds(g, 1), pl.ds(at, across)] * shrink[low]
                scales.append(jnp.broadcast_to(row, (chunk, across)).astype(BF16))
            for r in range(0, depth, chunk):
                words = slots[slot, r : r + chunk, column : column + across]
                for low in range(2):
                    level = (words & masks[low]).astype(F32).astype(BF16)
                    out_ref[
                        pl.ds(start + r, chunk),
                        low * quarter + column : low * quarter + column + across,
                    ] = (level - middles[low]) * scales[low]

        @pl.when(g + ahead < groups)
        def _():
            fetch(g + ahead).start()

        return carry

    lax.fori_loop(0, groups, step, 0)


def dequantize(half, code_words, group_scales):
    rows, quarter = code_words.shape
    groups = group_scales.shape[0]
    ahead = 8
    return pl.pallas_call(
        dequantize_kernel,
        in_specs=[
            pl.BlockSpec(memory_space=pltpu.SMEM),
            pl.BlockSpec(memory_space=pltpu.HBM),
            pl.BlockSpec(memory_space=pltpu.HBM),
        ],
        out_specs=pl.BlockSpec(memory_space=pltpu.VMEM),
        out_shape=pltpu.VMEM((rows, 2 * quarter), BF16),
        scratch_shapes=[
            pltpu.VMEM((ahead, rows // groups, quarter), jnp.int32),
            pltpu.VMEM(group_scales.shape, group_scales.dtype),
            pltpu.VMEM(group_scales.shape, F32),
            pltpu.SemaphoreType.DMA((ahead + 1,)),
        ],
        compiler_params=pltpu.CompilerParams(vmem_limit_bytes=12 * 1024 * 1024),
        cost_estimate=pl.CostEstimate(flops=rows * quarter * 15, bytes_accessed=rows * quarter * 8, transcendentals=0),
    )(half, in_hbm(code_words), in_hbm(group_scales))


def attend_kernel(first, last, blocks, after, tile, q_ref, *refs):
    kv_refs = refs[:blocks]
    refs = refs[blocks + after :]
    if not first:
        m_in, l_in, acc_in = refs[:3]
        refs = refs[3:]
    scale = LOG2E / math.sqrt(HD)
    groups, rows, width = q_ref.shape
    total = groups * rows
    queries = q_ref[...].reshape(total, width)
    keys, values = [], []
    for ref in kv_refs:
        count = ref.shape[0] * rows
        keys.append(ref[:, 0].reshape(count, width))
        values.append(ref[:, 1].reshape(count, width))

    def scores(step):
        row, block = divmod(step, blocks)
        return lax.dot_general(
            queries[row * tile : (row + 1) * tile],
            keys[block],
            (((1,), (1,)), ((), ())),
            preferred_element_type=F32,
        )

    steps = (total // tile) * blocks
    ahead = scores(0)
    for step in range(steps):
        row, block = divmod(step, blocks)
        here = slice(row * tile, (row + 1) * tile)
        s = ahead
        if step + 1 < steps:
            ahead = scores(step + 1)
        fresh = first and block == 0
        if block == 0 and not first:
            peak, total_l, acc = m_in[here, :], l_in[here, :], acc_in[here, :]
        s_peak = jnp.broadcast_to(jnp.max(s, axis=1, keepdims=True), (tile, width))
        new_peak = s_peak if fresh else jnp.maximum(peak, s_peak)
        parts, part_sum = [], None
        for lane in range(s.shape[1] // width):
            lifted = jnp.exp2((s[:, lane * width : (lane + 1) * width] - new_peak) * scale)
            part_sum = lifted if part_sum is None else part_sum + lifted
            parts.append(lifted.astype(BF16))
        mixed = jnp.dot(jnp.concatenate(parts, axis=1), values[block], preferred_element_type=F32)
        if fresh:
            total_l, acc = part_sum, mixed
        else:
            fade = jnp.exp2((peak - new_peak) * scale)
            total_l = total_l * fade + part_sum
            acc = acc * fade + mixed
        peak = new_peak
        if block == blocks - 1:
            if last:
                (out_ref,) = refs
                whole = jnp.sum(total_l, axis=1, keepdims=True)
                out_ref[here, :] = (acc / whole).astype(BF16)
            else:
                m_out, l_out, acc_out = refs
                m_out[here, :] = peak
                l_out[here, :] = total_l
                acc_out[here, :] = acc


def attend(queries, kv_blocks, state, last=False, after=(), tile=384):
    groups, rows, width = queries.shape
    total = groups * rows
    blocks = len(kv_blocks)
    first = state is None
    carried = jax.ShapeDtypeStruct((total, width), F32)
    out_shape = jax.ShapeDtypeStruct((total, width), BF16) if last else (carried,) * 3
    pairs = total * sum(block.shape[0] * rows for block in kv_blocks)
    return pl.pallas_call(
        functools.partial(attend_kernel, first, last, blocks, len(after), tile),
        out_shape=out_shape,
        compiler_params=pltpu.CompilerParams(vmem_limit_bytes=16 * 1024 * 1024),
        cost_estimate=pl.CostEstimate(
            flops=pairs * width * 4, bytes_accessed=total * width * 2 * (2 * blocks + 7), transcendentals=pairs
        ),
    )(queries, *kv_blocks, *after, *(() if first else state))


def project_kernel(tile, x_ref, w_ref, out_ref):
    x = jnp.concatenate([x_ref[h] for h in range(x_ref.shape[0])], axis=1)
    for c in range(0, out_ref.shape[1], tile):
        mixed = jnp.dot(x, w_ref[:, c : c + tile], preferred_element_type=F32)
        out_ref[:, c : c + tile] = mixed.astype(out_ref.dtype)


def project(returned, weights, out_type, tile=512):
    heads, tokens, width = returned.shape
    rows, columns = weights.shape
    return pl.pallas_call(
        functools.partial(project_kernel, tile),
        in_specs=[pl.BlockSpec(memory_space=pltpu.VMEM)] * 2,
        out_specs=pl.BlockSpec(memory_space=pltpu.VMEM),
        out_shape=jax.ShapeDtypeStruct((tokens, columns), out_type),
        compiler_params=pltpu.CompilerParams(vmem_limit_bytes=8 * 1024 * 1024),
        cost_estimate=pl.CostEstimate(
            flops=2 * tokens * rows * columns, bytes_accessed=rows * columns * 2, transcendentals=0
        ),
    )(returned, weights)


HEAD_AXES = ("zh", "zl", "yl")
RING = "x"


def body(head_inputs, positions, code_words, group_scales, out_gate, out_bias):
    ring = lax.axis_size(RING)
    half = lax.axis_index("yh").astype(jnp.int32).reshape(1)
    turned_queries, turned_pairs = rotate(positions, head_inputs)

    def regroup(a):
        return lax.all_to_all(a, HEAD_AXES, split_axis=0, concat_axis=0, tiled=True)

    def swap(a):
        return lax.ppermute(a, "c", [(0, 1), (1, 0)])

    def send(a, way):
        hops = []
        for i in range(ring):
            hops.append((2 * i, 2 * ((i + way) % ring)))
            hops.append((2 * i + 1, 2 * ((i - way) % ring) + 1))
        return lax.ppermute(a, (RING, "c"), hops)

    own = regroup(turned_pairs)
    theirs = dequantize(1 - half, code_words, group_scales)
    own, theirs, turned_queries = lax.optimization_barrier((own, theirs, turned_queries))
    near = send(own, 1)
    back = send(own, -1)
    queries = regroup(turned_queries)
    near, back, own = lax.optimization_barrier((near, back, own))
    far = send(back, -1)
    beside, near_beside, back_beside = swap(own), swap(near), swap(back)
    state = attend(queries, [own, near, back], None)
    state = attend(queries, [beside, near_beside, back_beside], state)
    far, state = lax.optimization_barrier((far, state))
    far_beside = swap(far)
    state = attend(queries, [far], state)
    attended = attend(queries, [far_beside], state, True)
    returned = regroup(attended.reshape(queries.shape))
    returned, half = lax.optimization_barrier((returned, half))
    mine = dequantize(half, code_words, group_scales)
    outgoing = project(returned, theirs, BF16)
    incoming = lax.ppermute(outgoing, "yh", [(0, 1), (1, 0)])
    kept = project(returned, mine, F32)
    return out_gate[None, :] * (kept + incoming.astype(F32) + out_bias[None, :])


def solution(mesh):
    x, blk, yh = mesh.devices.shape
    fine = Mesh(mesh.devices.reshape(x, blk // 8, 2, 2, 2, yh), ("x", "zh", "zl", "yl", "c", "yh"))
    tokens = ("x", "zh", "zl", "yl", "c")
    placed = (
        P(tokens, None, "yh", None),
        P(None, tokens),
        P("yh", None),
        P("yh", None),
        P("yh"),
        P("yh"),
    )
    return jax.shard_map(
        body, mesh=fine, in_specs=placed, out_specs=P(tokens, "yh"), check_vma=False
    )
```

```python
import functools
import math

import jax
import jax.numpy as jnp
from jax import lax
from jax.experimental import pallas as pl
from jax.experimental.pallas import tpu as pltpu
from jax.sharding import Mesh
from jax.sharding import PartitionSpec as P

HD = 128
LOG2E = 1.4426950408889634
F32 = jnp.float32
BF16 = jnp.bfloat16


def angle_rates(width):
    frame = (width - 4 * (width // 6)) // 2
    side = width // 6
    pair = lax.broadcasted_iota(jnp.int32, (3, width), 1) // 2
    row = lax.broadcasted_iota(jnp.int32, (3, width), 0)
    start = jnp.where(row == 0, 0, jnp.where(row == 1, frame, frame + side))
    extent = jnp.where(row == 0, frame, side)
    within = pair - start
    rate = jnp.exp(within.astype(F32) / extent.astype(F32) * (-math.log(10000.0)))
    return jnp.where((within >= 0) & (within < extent), rate, 0.0)


def rotate_kernel(pos_hbm, x_hbm, q_ref, kv_ref, pos_ref, x_ref, wide, sems):
    pos_copy = pltpu.make_async_copy(pos_hbm, pos_ref, sems.at[0])
    x_copy = pltpu.make_async_copy(x_hbm, x_ref, sems.at[1])
    pos_copy.start()
    x_copy.start()
    tokens, kinds, heads, width = x_ref.shape
    rates = angle_rates(width)
    is_even = lax.broadcasted_iota(jnp.int32, (tokens, width), 1) % 2 == 0
    pos_copy.wait()
    angles = lax.dot_general(
        pos_ref[...].astype(F32),
        rates,
        (((0,), (0,)), ((), ())),
        precision=lax.Precision.HIGHEST,
        preferred_element_type=F32,
    )
    cosine = jnp.cos(angles)
    sine = jnp.sin(angles)
    sine_even = jnp.where(is_even, -sine, 0.0)
    sine_odd = jnp.where(is_even, 0.0, sine)
    x_copy.wait()
    wide[: tokens * kinds * heads, :] = x_ref[...].astype(F32).reshape(tokens * kinds * heads, width)
    for kind in range(kinds):
        for head in range(heads):
            x = wide[pl.ds(kind * heads + head, tokens, stride=kinds * heads), :]
            if kind < 2:
                right = pltpu.roll(x, 1, 1)
                left = pltpu.roll(x, width - 1, 1)
                x = x * cosine + (left * sine_even + right * sine_odd)
            if kind:
                kv_ref[head, kind - 1] = x.astype(BF16)
            else:
                q_ref[head] = x.astype(BF16)


def rotate(positions, head_inputs):
    tokens, kinds, heads, width = head_inputs.shape
    return pl.pallas_call(
        rotate_kernel,
        in_specs=[pl.BlockSpec(memory_space=pltpu.HBM)] * 2,
        out_specs=[pl.BlockSpec(memory_space=pltpu.VMEM)] * 2,
        out_shape=[
            jax.ShapeDtypeStruct((heads, tokens, width), BF16),
            jax.ShapeDtypeStruct((heads, kinds - 1, tokens, width), BF16),
        ],
        scratch_shapes=[
            pltpu.VMEM(positions.shape, positions.dtype),
            pltpu.VMEM(head_inputs.shape, head_inputs.dtype),
            pltpu.VMEM(((tokens + 1) * kinds * heads, width), F32),
            pltpu.SemaphoreType.DMA((2,)),
        ],
        compiler_params=pltpu.CompilerParams(vmem_limit_bytes=16 * 1024 * 1024),
    )(in_hbm(positions), in_hbm(head_inputs))


def in_hbm(array):
    return pltpu.with_memory_space_constraint(array, pltpu.HBM)


def dequantize_kernel(half_ref, words_ref, scales_ref, out_ref, slots, narrow, wide, sems):
    rows, quarter = words_ref.shape
    groups = scales_ref.shape[0]
    depth = rows // groups
    half = half_ref[0]
    ahead, chunk, across = slots.shape[0], 16, 256

    def fetch(g):
        slot = lax.rem(g, ahead)
        start = pl.multiple_of(g * depth, depth)
        return pltpu.make_async_copy(words_ref.at[pl.ds(start, depth)], slots.at[slot], sems.at[slot])

    scales_copy = pltpu.make_async_copy(scales_ref, narrow, sems.at[ahead])
    scales_copy.start()
    for g in range(ahead):
        fetch(g).start()
    scales_copy.wait()
    wide[...] = narrow[...].astype(F32)

    upper = half == 1
    block = (chunk, across)
    masks = [jnp.full(block, jnp.where(upper, 3840 << (4 * low), 15 << (4 * low)), jnp.int32) for low in range(2)]
    middles = [
        jnp.full(block, jnp.where(upper, 2048.0 * 16**low, 8.0 * 16**low), F32).astype(BF16) for low in range(2)
    ]
    shrink = [jnp.where(upper, 0.00390625 / 16**low, 1.0 / 16**low) for low in range(2)]

    def step(g, carry):
        fetch(g).wait()
        slot = lax.rem(g, ahead)
        start = pl.multiple_of(g * depth, depth)
        for column in range(0, quarter, across):
            scales = []
            for low in range(2):
                at = pl.multiple_of((2 * half + low) * quarter + column, 128)
                row = wide[pl.ds(g, 1), pl.ds(at, across)] * shrink[low]
                scales.append(jnp.broadcast_to(row, (chunk, across)).astype(BF16))
            for r in range(0, depth, chunk):
                words = slots[slot, r : r + chunk, column : column + across]
                for low in range(2):
                    level = (words & masks[low]).astype(F32).astype(BF16)
                    out_ref[
                        pl.ds(start + r, chunk),
                        low * quarter + column : low * quarter + column + across,
                    ] = (level - middles[low]) * scales[low]

        @pl.when(g + ahead < groups)
        def _():
            fetch(g + ahead).start()

        return carry

    lax.fori_loop(0, groups, step, 0)


def dequantize(half, code_words, group_scales):
    rows, quarter = code_words.shape
    groups = group_scales.shape[0]
    ahead = 8
    return pl.pallas_call(
        dequantize_kernel,
        in_specs=[
            pl.BlockSpec(memory_space=pltpu.SMEM),
            pl.BlockSpec(memory_space=pltpu.HBM),
            pl.BlockSpec(memory_space=pltpu.HBM),
        ],
        out_specs=pl.BlockSpec(memory_space=pltpu.VMEM),
        out_shape=pltpu.VMEM((rows, 2 * quarter), BF16),
        scratch_shapes=[
            pltpu.VMEM((ahead, rows // groups, quarter), jnp.int32),
            pltpu.VMEM(group_scales.shape, group_scales.dtype),
            pltpu.VMEM(group_scales.shape, F32),
            pltpu.SemaphoreType.DMA((ahead + 1,)),
        ],
        compiler_params=pltpu.CompilerParams(vmem_limit_bytes=12 * 1024 * 1024),
        cost_estimate=pl.CostEstimate(flops=rows * quarter * 15, bytes_accessed=rows * quarter * 8, transcendentals=0),
    )(half, in_hbm(code_words), in_hbm(group_scales))


def keep_kernel(half_ref, words_ref, scales_ref, x_ref, out_ref, slots, narrow, wide, even, odd, x_pairs, sems):
    rows, quarter = words_ref.shape
    groups, depth = scales_ref.shape[0], rows // scales_ref.shape[0]
    half = half_ref[0]
    chunk, across, tile = 16, 256, 512
    scales_copy = pltpu.make_async_copy(scales_ref, narrow, sems.at[groups])
    scales_copy.start()

    def fetch(g):
        start = pl.multiple_of(g * depth, depth)
        return pltpu.make_async_copy(words_ref.at[pl.ds(start, depth)], slots.at[g], sems.at[g])

    for g in range(groups):
        fetch(g).start()
    for pair in range(groups // 2):
        x_pairs[pair] = jnp.concatenate([x_ref[2 * pair], x_ref[2 * pair + 1]], axis=1)
    out_ref[...] = jnp.zeros_like(out_ref)
    upper = half == 1
    block = (chunk, across)
    masks = [jnp.full(block, jnp.where(upper, 3840 << (4 * low), 15 << (4 * low)), jnp.int32) for low in range(2)]
    middles = [
        jnp.full(block, jnp.where(upper, 2048.0 * 16**low, 8.0 * 16**low), F32).astype(BF16) for low in range(2)
    ]
    shrink = [jnp.where(upper, 0.00390625 / 16**low, 1.0 / 16**low) for low in range(2)]
    scales_copy.wait()
    wide[...] = narrow[...].astype(F32)

    def unpack(pair, target):
        for member in range(2):
            g = 2 * pair + member
            fetch(g).wait()
            for column in range(0, quarter, across):
                scales = []
                for low in range(2):
                    at = pl.multiple_of((2 * half + low) * quarter + column, 128)
                    row = wide[pl.ds(g, 1), pl.ds(at, across)] * shrink[low]
                    scales.append(jnp.broadcast_to(row, block).astype(BF16))
                for r in range(0, depth, chunk):
                    words = slots[g, r : r + chunk, column : column + across]
                    for low in range(2):
                        level = (words & masks[low]).astype(F32).astype(BF16)
                        target[
                            member * depth + r : member * depth + r + chunk,
                            low * quarter + column : low * quarter + column + across,
                        ] = (level - middles[low]) * scales[low]

    def add(pair, source):
        x = x_pairs[pair]
        for c in range(0, out_ref.shape[1], tile):
            out_ref[:, c : c + tile] += jnp.dot(x, source[:, c : c + tile], preferred_element_type=F32)

    unpack(0, even)

    def step(i, carry):
        add(2 * i, even)
        unpack(2 * i + 1, odd)
        add(2 * i + 1, odd)
        unpack(2 * i + 2, even)
        return carry

    lax.fori_loop(0, groups // 4 - 1, step, 0)
    add(groups // 2 - 2, even)
    unpack(groups // 2 - 1, odd)
    add(groups // 2 - 1, odd)


def keep(half, code_words, group_scales, returned):
    rows, quarter = code_words.shape
    groups = group_scales.shape[0]
    heads, tokens, width = returned.shape
    return pl.pallas_call(
        keep_kernel,
        in_specs=[
            pl.BlockSpec(memory_space=pltpu.SMEM),
            pl.BlockSpec(memory_space=pltpu.HBM),
            pl.BlockSpec(memory_space=pltpu.HBM),
            pl.BlockSpec(memory_space=pltpu.VMEM),
        ],
        out_specs=pl.BlockSpec(memory_space=pltpu.VMEM),
        out_shape=jax.ShapeDtypeStruct((tokens, 2 * quarter), F32),
        scratch_shapes=[
            pltpu.VMEM((groups, rows // groups, quarter), jnp.int32),
            pltpu.VMEM(group_scales.shape, group_scales.dtype),
            pltpu.VMEM(group_scales.shape, F32),
            pltpu.VMEM((2 * width, 2 * quarter), BF16),
            pltpu.VMEM((2 * width, 2 * quarter), BF16),
            pltpu.VMEM((heads // 2, tokens, 2 * width), BF16),
            pltpu.SemaphoreType.DMA((groups + 1,)),
        ],
        compiler_params=pltpu.CompilerParams(vmem_limit_bytes=20 * 1024 * 1024),
        cost_estimate=pl.CostEstimate(
            flops=4 * tokens * rows * quarter, bytes_accessed=rows * quarter * 8, transcendentals=0
        ),
    )(half, in_hbm(code_words), in_hbm(group_scales), returned)


def attend_kernel(first, last, blocks, after, tile, q_ref, *refs):
    kv_refs = refs[:blocks]
    refs = refs[blocks + after :]
    if not first:
        m_in, l_in, acc_in = refs[:3]
        refs = refs[3:]
    scale = LOG2E / math.sqrt(HD)
    groups, rows, width = q_ref.shape
    total = groups * rows
    queries = q_ref[...].reshape(total, width)
    keys, values = [], []
    for ref in kv_refs:
        count = ref.shape[0] * rows
        keys.append(ref[:, 0].reshape(count, width))
        values.append(ref[:, 1].reshape(count, width))

    def scores(step):
        row, block = divmod(step, blocks)
        return lax.dot_general(
            queries[row * tile : (row + 1) * tile],
            keys[block],
            (((1,), (1,)), ((), ())),
            preferred_element_type=F32,
        )

    steps = (total // tile) * blocks
    ahead = scores(0)
    for step in range(steps):
        row, block = divmod(step, blocks)
        here = slice(row * tile, (row + 1) * tile)
        s = ahead
        if step + 1 < steps:
            ahead = scores(step + 1)
        fresh = first and block == 0
        if block == 0 and not first:
            peak, total_l, acc = m_in[here, :], l_in[here, :], acc_in[here, :]
        s_peak = jnp.broadcast_to(jnp.max(s, axis=1, keepdims=True), (tile, width))
        new_peak = s_peak if fresh else jnp.maximum(peak, s_peak)
        parts, part_sum = [], None
        for lane in range(s.shape[1] // width):
            lifted = jnp.exp2((s[:, lane * width : (lane + 1) * width] - new_peak) * scale)
            part_sum = lifted if part_sum is None else part_sum + lifted
            parts.append(lifted.astype(BF16))
        mixed = jnp.dot(jnp.concatenate(parts, axis=1), values[block], preferred_element_type=F32)
        if fresh:
            total_l, acc = part_sum, mixed
        else:
            fade = jnp.exp2((peak - new_peak) * scale)
            total_l = total_l * fade + part_sum
            acc = acc * fade + mixed
        peak = new_peak
        if block == blocks - 1:
            if last:
                (out_ref,) = refs
                whole = jnp.sum(total_l, axis=1, keepdims=True)
                out_ref[here, :] = (acc / whole).astype(BF16)
            else:
                m_out, l_out, acc_out = refs
                m_out[here, :] = peak
                l_out[here, :] = total_l
                acc_out[here, :] = acc


def attend(queries, kv_blocks, state, last=False, after=(), tile=384):
    groups, rows, width = queries.shape
    total = groups * rows
    blocks = len(kv_blocks)
    first = state is None
    carried = jax.ShapeDtypeStruct((total, width), F32)
    out_shape = jax.ShapeDtypeStruct((total, width), BF16) if last else (carried,) * 3
    pairs = total * sum(block.shape[0] * rows for block in kv_blocks)
    return pl.pallas_call(
        functools.partial(attend_kernel, first, last, blocks, len(after), tile),
        out_shape=out_shape,
        compiler_params=pltpu.CompilerParams(vmem_limit_bytes=16 * 1024 * 1024),
        cost_estimate=pl.CostEstimate(
            flops=pairs * width * 4, bytes_accessed=total * width * 2 * (2 * blocks + 7), transcendentals=pairs
        ),
    )(queries, *kv_blocks, *after, *(() if first else state))


def project_kernel(tile, x_ref, w_ref, out_ref):
    x = jnp.concatenate([x_ref[h] for h in range(x_ref.shape[0])], axis=1)
    for c in range(0, out_ref.shape[1], tile):
        mixed = jnp.dot(x, w_ref[:, c : c + tile], preferred_element_type=F32)
        out_ref[:, c : c + tile] = mixed.astype(out_ref.dtype)


def project(returned, weights, out_type, tile=512):
    heads, tokens, width = returned.shape
    rows, columns = weights.shape
    return pl.pallas_call(
        functools.partial(project_kernel, tile),
        in_specs=[pl.BlockSpec(memory_space=pltpu.VMEM)] * 2,
        out_specs=pl.BlockSpec(memory_space=pltpu.VMEM),
        out_shape=jax.ShapeDtypeStruct((tokens, columns), out_type),
        compiler_params=pltpu.CompilerParams(vmem_limit_bytes=8 * 1024 * 1024),
        cost_estimate=pl.CostEstimate(
            flops=2 * tokens * rows * columns, bytes_accessed=rows * columns * 2, transcendentals=0
        ),
    )(returned, weights)


HEAD_AXES = ("zh", "zl", "yl")
RING = "x"


def body(head_inputs, positions, code_words, group_scales, out_gate, out_bias):
    ring = lax.axis_size(RING)
    half = lax.axis_index("yh").astype(jnp.int32).reshape(1)
    turned_queries, turned_pairs = rotate(positions, head_inputs)

    def regroup(a):
        return lax.all_to_all(a, HEAD_AXES, split_axis=0, concat_axis=0, tiled=True)

    def swap(a):
        return lax.ppermute(a, "c", [(0, 1), (1, 0)])

    def send(a, way):
        hops = []
        for i in range(ring):
            hops.append((2 * i, 2 * ((i + way) % ring)))
            hops.append((2 * i + 1, 2 * ((i - way) % ring) + 1))
        return lax.ppermute(a, (RING, "c"), hops)

    own = regroup(turned_pairs)
    theirs = dequantize(1 - half, code_words, group_scales)
    own, theirs, turned_queries = lax.optimization_barrier((own, theirs, turned_queries))
    near = send(own, 1)
    back = send(own, -1)
    queries = regroup(turned_queries)
    near, back, own = lax.optimization_barrier((near, back, own))
    far = send(back, -1)
    beside, near_beside, back_beside = swap(own), swap(near), swap(back)
    state = attend(queries, [own, near, back], None)
    state = attend(queries, [beside, near_beside, back_beside], state)
    far, state = lax.optimization_barrier((far, state))
    far_beside = swap(far)
    state = attend(queries, [far], state)
    attended = attend(queries, [far_beside], state, True)
    returned = regroup(attended.reshape(queries.shape))
    returned, half = lax.optimization_barrier((returned, half))
    outgoing = project(returned, theirs, BF16)
    incoming = lax.ppermute(outgoing, "yh", [(0, 1), (1, 0)])
    kept = keep(half, code_words, group_scales, returned)
    return out_gate[None, :] * (kept + incoming.astype(F32) + out_bias[None, :])


def solution(mesh):
    x, blk, yh = mesh.devices.shape
    fine = Mesh(mesh.devices.reshape(x, blk // 8, 2, 2, 2, yh), ("x", "zh", "zl", "yl", "c", "yh"))
    tokens = ("x", "zh", "zl", "yl", "c")
    placed = (
        P(tokens, None, "yh", None),
        P(None, tokens),
        P("yh", None),
        P("yh", None),
        P("yh"),
        P("yh"),
    )
    return jax.shard_map(
        body, mesh=fine, in_specs=placed, out_specs=P(tokens, "yh"), check_vma=False
    )
```

```python
import functools
import math

import jax
import jax.numpy as jnp
from jax import lax
from jax.experimental import pallas as pl
from jax.experimental.pallas import tpu as pltpu
from jax.sharding import Mesh
from jax.sharding import PartitionSpec as P

HD = 128
LOG2E = 1.4426950408889634
F32 = jnp.float32
BF16 = jnp.bfloat16


def angle_rates(width):
    frame = (width - 4 * (width // 6)) // 2
    side = width // 6
    pair = lax.broadcasted_iota(jnp.int32, (3, width), 1) // 2
    row = lax.broadcasted_iota(jnp.int32, (3, width), 0)
    start = jnp.where(row == 0, 0, jnp.where(row == 1, frame, frame + side))
    extent = jnp.where(row == 0, frame, side)
    within = pair - start
    rate = jnp.exp(within.astype(F32) / extent.astype(F32) * (-math.log(10000.0)))
    return jnp.where((within >= 0) & (within < extent), rate, 0.0)


def rotate_kernel(pos_hbm, x_hbm, q_ref, kv_ref, pos_ref, x_ref, wide, sems):
    pos_copy = pltpu.make_async_copy(pos_hbm, pos_ref, sems.at[0])
    x_copy = pltpu.make_async_copy(x_hbm, x_ref, sems.at[1])
    pos_copy.start()
    x_copy.start()
    tokens, kinds, heads, width = x_ref.shape
    rates = angle_rates(width)
    is_even = lax.broadcasted_iota(jnp.int32, (tokens, width), 1) % 2 == 0
    pos_copy.wait()
    angles = lax.dot_general(
        pos_ref[...].astype(F32),
        rates,
        (((0,), (0,)), ((), ())),
        precision=lax.Precision.HIGHEST,
        preferred_element_type=F32,
    )
    cosine = jnp.cos(angles)
    sine = jnp.sin(angles)
    sine_even = jnp.where(is_even, -sine, 0.0)
    sine_odd = jnp.where(is_even, 0.0, sine)
    x_copy.wait()
    wide[: tokens * kinds * heads, :] = x_ref[...].astype(F32).reshape(tokens * kinds * heads, width)
    for kind in range(kinds):
        for head in range(heads):
            x = wide[pl.ds(kind * heads + head, tokens, stride=kinds * heads), :]
            if kind < 2:
                right = pltpu.roll(x, 1, 1)
                left = pltpu.roll(x, width - 1, 1)
                x = x * cosine + (left * sine_even + right * sine_odd)
            if kind:
                kv_ref[head, kind - 1] = x.astype(BF16)
            else:
                q_ref[head] = x.astype(BF16)


def rotate(positions, head_inputs):
    tokens, kinds, heads, width = head_inputs.shape
    return pl.pallas_call(
        rotate_kernel,
        in_specs=[pl.BlockSpec(memory_space=pltpu.HBM)] * 2,
        out_specs=[pl.BlockSpec(memory_space=pltpu.VMEM)] * 2,
        out_shape=[
            jax.ShapeDtypeStruct((heads, tokens, width), BF16),
            jax.ShapeDtypeStruct((heads, kinds - 1, tokens, width), BF16),
        ],
        scratch_shapes=[
            pltpu.VMEM(positions.shape, positions.dtype),
            pltpu.VMEM(head_inputs.shape, head_inputs.dtype),
            pltpu.VMEM(((tokens + 1) * kinds * heads, width), F32),
            pltpu.SemaphoreType.DMA((2,)),
        ],
        compiler_params=pltpu.CompilerParams(vmem_limit_bytes=16 * 1024 * 1024),
    )(in_hbm(positions), in_hbm(head_inputs))


def in_hbm(array):
    return pltpu.with_memory_space_constraint(array, pltpu.HBM)


def dequantize_kernel(half_ref, words_ref, scales_ref, out_ref, slots, narrow, wide, sems):
    rows, quarter = words_ref.shape
    groups = scales_ref.shape[0]
    depth = rows // groups
    half = half_ref[0]
    ahead, chunk, across = slots.shape[0], 16, 256

    def fetch(g):
        slot = lax.rem(g, ahead)
        start = pl.multiple_of(g * depth, depth)
        return pltpu.make_async_copy(words_ref.at[pl.ds(start, depth)], slots.at[slot], sems.at[slot])

    scales_copy = pltpu.make_async_copy(scales_ref, narrow, sems.at[ahead])
    scales_copy.start()
    for g in range(ahead):
        fetch(g).start()
    scales_copy.wait()
    wide[...] = narrow[...].astype(F32)

    upper = half == 1
    block = (chunk, across)
    masks = [jnp.full(block, jnp.where(upper, 3840 << (4 * low), 15 << (4 * low)), jnp.int32) for low in range(2)]
    middles = [
        jnp.full(block, jnp.where(upper, 2048.0 * 16**low, 8.0 * 16**low), F32).astype(BF16) for low in range(2)
    ]
    shrink = [jnp.where(upper, 0.00390625 / 16**low, 1.0 / 16**low) for low in range(2)]

    def step(g, carry):
        fetch(g).wait()
        slot = lax.rem(g, ahead)
        start = pl.multiple_of(g * depth, depth)
        for column in range(0, quarter, across):
            scales = []
            for low in range(2):
                at = pl.multiple_of((2 * half + low) * quarter + column, 128)
                row = wide[pl.ds(g, 1), pl.ds(at, across)] * shrink[low]
                scales.append(jnp.broadcast_to(row, (chunk, across)).astype(BF16))
            for r in range(0, depth, chunk):
                words = slots[slot, r : r + chunk, column : column + across]
                for low in range(2):
                    level = (words & masks[low]).astype(F32).astype(BF16)
                    out_ref[
                        pl.ds(start + r, chunk),
                        low * quarter + column : low * quarter + column + across,
                    ] = (level - middles[low]) * scales[low]

        @pl.when(g + ahead < groups)
        def _():
            fetch(g + ahead).start()

        return carry

    lax.fori_loop(0, groups, step, 0)


def dequantize(half, code_words, group_scales):
    rows, quarter = code_words.shape
    groups = group_scales.shape[0]
    ahead = 8
    return pl.pallas_call(
        dequantize_kernel,
        in_specs=[
            pl.BlockSpec(memory_space=pltpu.SMEM),
            pl.BlockSpec(memory_space=pltpu.HBM),
            pl.BlockSpec(memory_space=pltpu.HBM),
        ],
        out_specs=pl.BlockSpec(memory_space=pltpu.VMEM),
        out_shape=pltpu.VMEM((rows, 2 * quarter), BF16),
        scratch_shapes=[
            pltpu.VMEM((ahead, rows // groups, quarter), jnp.int32),
            pltpu.VMEM(group_scales.shape, group_scales.dtype),
            pltpu.VMEM(group_scales.shape, F32),
            pltpu.SemaphoreType.DMA((ahead + 1,)),
        ],
        compiler_params=pltpu.CompilerParams(vmem_limit_bytes=12 * 1024 * 1024),
        cost_estimate=pl.CostEstimate(flops=rows * quarter * 15, bytes_accessed=rows * quarter * 8, transcendentals=0),
    )(half, in_hbm(code_words), in_hbm(group_scales))


def keep_kernel(half_ref, words_ref, scales_ref, x_ref, gate_ref, bias_ref, out_ref, slots, narrow, wide, even, odd, x_pairs, sems):
    rows, quarter = words_ref.shape
    groups, depth = scales_ref.shape[0], rows // scales_ref.shape[0]
    half = half_ref[0]
    chunk, across, tile = 16, 256, 512
    scales_copy = pltpu.make_async_copy(scales_ref, narrow, sems.at[groups])
    scales_copy.start()

    def fetch(g):
        start = pl.multiple_of(g * depth, depth)
        return pltpu.make_async_copy(words_ref.at[pl.ds(start, depth)], slots.at[g], sems.at[g])

    for g in range(groups):
        fetch(g).start()
    for pair in range(groups // 2):
        x_pairs[pair] = jnp.concatenate([x_ref[2 * pair], x_ref[2 * pair + 1]], axis=1)
    out_ref[...] = jnp.zeros_like(out_ref)
    upper = half == 1
    block = (chunk, across)
    masks = [jnp.full(block, jnp.where(upper, 3840 << (4 * low), 15 << (4 * low)), jnp.int32) for low in range(2)]
    middles = [
        jnp.full(block, jnp.where(upper, 2048.0 * 16**low, 8.0 * 16**low), F32).astype(BF16) for low in range(2)
    ]
    shrink = [jnp.where(upper, 0.00390625 / 16**low, 1.0 / 16**low) for low in range(2)]
    scales_copy.wait()
    wide[...] = narrow[...].astype(F32)

    def unpack(pair, target):
        for member in range(2):
            g = 2 * pair + member
            fetch(g).wait()
            for column in range(0, quarter, across):
                scales = []
                for low in range(2):
                    at = pl.multiple_of((2 * half + low) * quarter + column, 128)
                    row = wide[pl.ds(g, 1), pl.ds(at, across)] * shrink[low]
                    scales.append(jnp.broadcast_to(row, block).astype(BF16))
                for r in range(0, depth, chunk):
                    words = slots[g, r : r + chunk, column : column + across]
                    for low in range(2):
                        level = (words & masks[low]).astype(F32).astype(BF16)
                        target[
                            member * depth + r : member * depth + r + chunk,
                            low * quarter + column : low * quarter + column + across,
                        ] = (level - middles[low]) * scales[low]

    def add(pair, source):
        x = x_pairs[pair]
        for c in range(0, out_ref.shape[1], tile):
            out_ref[:, c : c + tile] += jnp.dot(x, source[:, c : c + tile], preferred_element_type=F32)

    unpack(0, even)

    def step(i, carry):
        add(2 * i, even)
        unpack(2 * i + 1, odd)
        add(2 * i + 1, odd)
        unpack(2 * i + 2, even)
        return carry

    lax.fori_loop(0, groups // 4 - 1, step, 0)
    add(groups // 2 - 2, even)
    unpack(groups // 2 - 1, odd)
    add(groups // 2 - 1, odd)
    out_ref[...] = gate_ref[...] * (out_ref[...] + bias_ref[...])


def keep(half, code_words, group_scales, returned, out_gate, out_bias):
    rows, quarter = code_words.shape
    groups = group_scales.shape[0]
    heads, tokens, width = returned.shape
    return pl.pallas_call(
        keep_kernel,
        in_specs=[
            pl.BlockSpec(memory_space=pltpu.SMEM),
            pl.BlockSpec(memory_space=pltpu.HBM),
            pl.BlockSpec(memory_space=pltpu.HBM),
            pl.BlockSpec(memory_space=pltpu.VMEM),
            pl.BlockSpec(memory_space=pltpu.VMEM),
            pl.BlockSpec(memory_space=pltpu.VMEM),
        ],
        out_specs=pl.BlockSpec(memory_space=pltpu.VMEM),
        out_shape=jax.ShapeDtypeStruct((tokens, 2 * quarter), F32),
        scratch_shapes=[
            pltpu.VMEM((groups, rows // groups, quarter), jnp.int32),
            pltpu.VMEM(group_scales.shape, group_scales.dtype),
            pltpu.VMEM(group_scales.shape, F32),
            pltpu.VMEM((2 * width, 2 * quarter), BF16),
            pltpu.VMEM((2 * width, 2 * quarter), BF16),
            pltpu.VMEM((heads // 2, tokens, 2 * width), BF16),
            pltpu.SemaphoreType.DMA((groups + 1,)),
        ],
        compiler_params=pltpu.CompilerParams(vmem_limit_bytes=20 * 1024 * 1024),
        cost_estimate=pl.CostEstimate(
            flops=4 * tokens * rows * quarter, bytes_accessed=rows * quarter * 8, transcendentals=0
        ),
    )(half, in_hbm(code_words), in_hbm(group_scales), returned, out_gate[None, :], out_bias[None, :])


def attend_kernel(first, last, blocks, after, tile, q_ref, *refs):
    kv_refs = refs[:blocks]
    refs = refs[blocks + after :]
    if not first:
        m_in, l_in, acc_in = refs[:3]
        refs = refs[3:]
    scale = LOG2E / math.sqrt(HD)
    groups, rows, width = q_ref.shape
    total = groups * rows
    queries = q_ref[...].reshape(total, width)
    keys, values = [], []
    for ref in kv_refs:
        count = ref.shape[0] * rows
        keys.append(ref[:, 0].reshape(count, width))
        values.append(ref[:, 1].reshape(count, width))

    def scores(step):
        row, block = divmod(step, blocks)
        return lax.dot_general(
            queries[row * tile : (row + 1) * tile],
            keys[block],
            (((1,), (1,)), ((), ())),
            preferred_element_type=F32,
        )

    steps = (total // tile) * blocks
    ahead = scores(0)
    for step in range(steps):
        row, block = divmod(step, blocks)
        here = slice(row * tile, (row + 1) * tile)
        s = ahead
        if step + 1 < steps:
            ahead = scores(step + 1)
        fresh = first and block == 0
        if block == 0 and not first:
            peak, total_l, acc = m_in[here, :], l_in[here, :], acc_in[here, :]
        s_peak = jnp.broadcast_to(jnp.max(s, axis=1, keepdims=True), (tile, width))
        new_peak = s_peak if fresh else jnp.maximum(peak, s_peak)
        parts, part_sum = [], None
        for lane in range(s.shape[1] // width):
            lifted = jnp.exp2((s[:, lane * width : (lane + 1) * width] - new_peak) * scale)
            part_sum = lifted if part_sum is None else part_sum + lifted
            parts.append(lifted.astype(BF16))
        mixed = jnp.dot(jnp.concatenate(parts, axis=1), values[block], preferred_element_type=F32)
        if fresh:
            total_l, acc = part_sum, mixed
        else:
            fade = jnp.exp2((peak - new_peak) * scale)
            total_l = total_l * fade + part_sum
            acc = acc * fade + mixed
        peak = new_peak
        if block == blocks - 1:
            if last:
                (out_ref,) = refs
                whole = jnp.sum(total_l, axis=1, keepdims=True)
                out_ref[here, :] = (acc / whole).astype(BF16)
            else:
                m_out, l_out, acc_out = refs
                m_out[here, :] = peak
                l_out[here, :] = total_l
                acc_out[here, :] = acc


def attend(queries, kv_blocks, state, last=False, after=(), tile=384):
    groups, rows, width = queries.shape
    total = groups * rows
    blocks = len(kv_blocks)
    first = state is None
    carried = jax.ShapeDtypeStruct((total, width), F32)
    out_shape = jax.ShapeDtypeStruct((total, width), BF16) if last else (carried,) * 3
    pairs = total * sum(block.shape[0] * rows for block in kv_blocks)
    return pl.pallas_call(
        functools.partial(attend_kernel, first, last, blocks, len(after), tile),
        out_shape=out_shape,
        compiler_params=pltpu.CompilerParams(vmem_limit_bytes=16 * 1024 * 1024),
        cost_estimate=pl.CostEstimate(
            flops=pairs * width * 4, bytes_accessed=total * width * 2 * (2 * blocks + 7), transcendentals=pairs
        ),
    )(queries, *kv_blocks, *after, *(() if first else state))


def project_kernel(tile, x_ref, w_ref, out_ref):
    x = jnp.concatenate([x_ref[h] for h in range(x_ref.shape[0])], axis=1)
    for c in range(0, out_ref.shape[1], tile):
        mixed = jnp.dot(x, w_ref[:, c : c + tile], preferred_element_type=F32)
        out_ref[:, c : c + tile] = mixed.astype(out_ref.dtype)


def project(returned, weights, out_type, tile=512):
    heads, tokens, width = returned.shape
    rows, columns = weights.shape
    return pl.pallas_call(
        functools.partial(project_kernel, tile),
        in_specs=[pl.BlockSpec(memory_space=pltpu.VMEM)] * 2,
        out_specs=pl.BlockSpec(memory_space=pltpu.VMEM),
        out_shape=jax.ShapeDtypeStruct((tokens, columns), out_type),
        compiler_params=pltpu.CompilerParams(vmem_limit_bytes=8 * 1024 * 1024),
        cost_estimate=pl.CostEstimate(
            flops=2 * tokens * rows * columns, bytes_accessed=rows * columns * 2, transcendentals=0
        ),
    )(returned, weights)


HEAD_AXES = ("zh", "zl", "yl")
RING = "x"


def body(head_inputs, positions, code_words, group_scales, out_gate, out_bias):
    ring = lax.axis_size(RING)
    half = lax.axis_index("yh").astype(jnp.int32).reshape(1)
    turned_queries, turned_pairs = rotate(positions, head_inputs)

    def regroup(a):
        return lax.all_to_all(a, HEAD_AXES, split_axis=0, concat_axis=0, tiled=True)

    def swap(a):
        return lax.ppermute(a, "c", [(0, 1), (1, 0)])

    def send(a, way):
        hops = []
        for i in range(ring):
            hops.append((2 * i, 2 * ((i + way) % ring)))
            hops.append((2 * i + 1, 2 * ((i - way) % ring) + 1))
        return lax.ppermute(a, (RING, "c"), hops)

    own = regroup(turned_pairs)
    theirs = dequantize(1 - half, code_words, group_scales)
    own, theirs, turned_queries = lax.optimization_barrier((own, theirs, turned_queries))
    near = send(own, 1)
    back = send(own, -1)
    queries = regroup(turned_queries)
    near, back, own = lax.optimization_barrier((near, back, own))
    far = send(back, -1)
    beside, near_beside, back_beside = swap(own), swap(near), swap(back)
    state = attend(queries, [own, near, back], None)
    state = attend(queries, [beside, near_beside, back_beside], state)
    far, state = lax.optimization_barrier((far, state))
    far_beside = swap(far)
    state = attend(queries, [far], state)
    attended = attend(queries, [far_beside], state, True)
    returned = regroup(attended.reshape(queries.shape))
    returned, half = lax.optimization_barrier((returned, half))
    outgoing = project(returned, theirs, BF16)
    incoming = lax.ppermute(outgoing, "yh", [(0, 1), (1, 0)])
    kept = keep(half, code_words, group_scales, returned, out_gate, out_bias)
    return kept + out_gate[None, :] * incoming.astype(F32)


def solution(mesh):
    x, blk, yh = mesh.devices.shape
    fine = Mesh(mesh.devices.reshape(x, blk // 8, 2, 2, 2, yh), ("x", "zh", "zl", "yl", "c", "yh"))
    tokens = ("x", "zh", "zl", "yl", "c")
    placed = (
        P(tokens, None, "yh", None),
        P(None, tokens),
        P("yh", None),
        P("yh", None),
        P("yh"),
        P("yh"),
    )
    return jax.shard_map(
        body, mesh=fine, in_specs=placed, out_specs=P(tokens, "yh"), check_vma=False
    )
```
